128 devices in a mesh: tile: 16 (over z, y), slide: 8 (over x, core).
Axes of the slice: x: 4, y: 4, z: 4, core: 2. Of those that a mesh axis runs over, the one named last changes fastest.
Arguments:
- features_in: bfloat16 [4096, 49, 2048], P(('tile', 'slide')), may hold values from -12 to 12
- w_reduce: bfloat16 [2048, 512], replicated, may hold values from -0.125 to 0.125
- w_expand: bfloat16 [512, 2048], replicated, may hold values from -0.25 to 0.25
- att_value: bfloat16 [2048, 1024], replicated, may hold values from -0.125 to 0.125
- att_gate: bfloat16 [2048, 1024], replicated, may hold values from -0.125 to 0.125
- att_vector: float32 [1024], replicated, may hold values from -0.07 to 0.07
- classifier: float32 [2048], replicated, may hold values from -0.125 to 0.125
- tile_slide: int32 [4096, 1], P(('tile', 'slide')), may hold values from 0 to 7; in each aligned block of 32 rows (0 to 31, 32 to 63, ...) at most 8 rows name the same one
- labels: int32 [8], P('slide'), may hold values from 0 to 1
Outputs:
- update_reduce: bfloat16 [2048, 512], replicated
- update_expand: bfloat16 [512, 2048], replicated
- slide_logits: float32 [8], P('slide')
- total_loss: float32 [], replicated
The draws below stay inside these ranges and needn't reach their ends.
Inputs may be any that keep to these rules, and one draw needn't show every extreme that they name: `tile_slide`: among the 32 tiles of one device at most 8 belong to one slide, and that many do on some device; every slide has tiles.
All inputs are finite; a program needn't handle non-finite values.
Results may differ from the reference program's by a relative error of at most 0.012.
Values may be sent and summed in bfloat16 or wider, within the bound.
A program may use at most 192 MiB of HBM per device.

```python
import math
from functools import partial
import jax
import jax.numpy as jnp
import numpy as np
from jax import lax

D = 2048
MID = 512
POS = 49
ATT = 1024
TILE_DEV = 32
TILES = 4096
SLIDES = 8
CAP = 8


def draw_features_in(key, part):
    key = jax.random.fold_in(key, 7)
    first, second = jax.random.split(key, 2)
    local_part = jax.random.normal(first, (TILES, POS, D), jnp.float32)
    common_part = jax.random.normal(second, (TILES, 1, D), jnp.float32)
    values = local_part + common_part
    return jnp.clip(values, -12.0, 12.0).astype(jnp.bfloat16)


def touch_ends(array, rng, smallest, high):
    longest = array.shape.index(max(array.shape))
    spots = []
    for shift in (0, 1):
        where = [jax.random.randint(jax.random.fold_in(rng, axis), (), 0, length) for axis, length in enumerate(array.shape)]
        where[longest] = (where[longest] + shift) % array.shape[longest]
        spots.append(tuple(where))
    return array.at[spots[0]].set(smallest).at[spots[1]].set(high)


def deal_out(key, own, number, rows, amount, top, bound, slope):
    order = jax.random.permutation(key, amount)
    crowded, usual = load_shares(amount, rows * top, bound, slope, True), load_shares(amount, rows * top, bound, slope, False)
    places = jnp.arange(amount)

    def named(lengths, offset_by):
        used = int((lengths > 0).sum())
        fixed = max(1, used // 4)
        shifted = fixed + (places - fixed + offset_by * (used - fixed)) % max(1, amount - fixed)
        return jnp.zeros((amount,), jnp.int32).at[order[jnp.where(places < fixed, places, shifted)]].set(jnp.asarray(lengths, jnp.int32))

    lengths = jnp.where(number % 4 == 0, named(crowded, number // 4), named(usual, number - number // 4 - 1))
    mixed = jax.random.permutation(jax.random.fold_in(own, 3), amount)
    giver, taker = mixed[0:amount // 2 * 2:2], mixed[1:amount // 2 * 2:2]
    room = jnp.minimum(lengths[giver] - 1, bound - lengths[taker]) // 2
    room = jnp.where((giver == order[0]) | (taker == order[0]) | (lengths[taker] == 0), 0, jnp.maximum(room, 0))
    shifted = jax.random.randint(jax.random.fold_in(own, 4), (amount // 2,), 0, 1 << 20) % (room + 1)
    lengths = lengths.at[giver].add(-shifted).at[taker].add(shifted)
    members = jnp.searchsorted(jnp.cumsum(lengths), jnp.arange(rows * top), side="right").astype(jnp.int32)
    grid = members.reshape(top, rows).T
    grid = grid[jax.random.permutation(jax.random.fold_in(own, 1), rows)]
    offset_by = jax.random.randint(jax.random.fold_in(own, 2), (rows, 1), 0, top)
    return jnp.take_along_axis(grid, (jnp.arange(top)[None, :] + offset_by) % top, axis=1)


def load_shares(number_of, total, limit, slope, full):
    weights = [(1 << 20) // math.isqrt(rank ** slope) + 1 for rank in range(1, number_of + 1)]
    largest = limit if full else min(limit, max(-(-total // number_of), total * weights[0] // sum(weights)))
    least = 1 if total - largest >= number_of - 1 else 0
    given, spare = [largest] + [least] * (number_of - 1), total - largest - least * (number_of - 1)
    while spare > 0:
        movable = [i for i in range(1, number_of) if given[i] < largest] or [i for i in range(1, number_of) if given[i] < limit]
        pool, remaining = sum([weights[i] for i in movable]), spare
        for i in movable:
            addition = min(limit - given[i], max(1, remaining * weights[i] // pool), spare)
            given[i] = given[i] + addition
            spare = spare - addition
    return np.array(given)


def bell_draw(rng, shape, spread, reach, held_as=jnp.bfloat16):
    result = spread * jax.random.normal(rng, shape, jnp.float32)
    return jnp.clip(result, min=-reach, max=reach).astype(held_as)


def setup_inputs(seed: int = 0) -> dict:
    seeds = jax.random.split(jax.random.key(seed), 10)
    features_in = draw_features_in(jax.random.fold_in(seeds[9], 71), 0)
    w_reduce = bell_draw(seeds[1], (D, MID), D ** -0.5, 0.125)
    w_expand = bell_draw(seeds[2], (MID, D), MID ** -0.5, 0.25)
    att_value = bell_draw(seeds[3], (D, ATT), D ** -0.5, 0.125)
    att_gate = bell_draw(seeds[4], (D, ATT), D ** -0.5, 0.125)
    att_vector = jnp.clip(jax.random.uniform(seeds[5], (ATT,), jnp.float32, -0.07, 0.07), -0.07, 0.07)
    classifier = bell_draw(seeds[6], (D,), D ** -0.5, 0.125, jnp.float32)
    tile_slide_keys = jax.random.split(jax.random.fold_in(seeds[7], 1), TILES // TILE_DEV)
    tile_slide_turns = jax.random.permutation(jax.random.fold_in(seeds[7], 3), TILES // TILE_DEV)
    tile_slide = jax.vmap(lambda own, number: deal_out(jax.random.fold_in(seeds[7], 2), own, number, TILE_DEV, SLIDES, 1, CAP, 2))(tile_slide_keys, tile_slide_turns).reshape((TILES, 1))
    labels = touch_ends(jax.random.randint(seeds[8], (SLIDES,), 0, 2), jax.random.fold_in(seeds[8], 1), 0, 1).astype(jnp.int32)
    return dict(features_in=features_in, w_reduce=w_reduce, w_expand=w_expand, att_value=att_value, att_gate=att_gate, att_vector=att_vector, classifier=classifier, tile_slide=tile_slide, labels=labels)


LOSS_SCALE = 1024.0

def score_exact(rows, att_value, att_gate, att_vector):
    value_proj = jnp.dot(rows, att_value.astype(jnp.float32), precision=lax.Precision.HIGHEST)
    gate_proj = jnp.dot(rows, att_gate.astype(jnp.float32), precision=lax.Precision.HIGHEST)
    return jnp.dot(jnp.tanh(value_proj) * jax.nn.sigmoid(gate_proj), att_vector, precision=lax.Precision.HIGHEST)

def pool_slides(features, att_value, att_gate, att_vector, classifier, member, label_values):
    scores = score_exact(features, att_value, att_gate, att_vector)
    weights = jnp.exp(scores)[:, None] * member
    weight_total = lax.optimization_barrier(jnp.sum(weights, axis=0))
    pooled = jnp.dot(weights.T, features, precision=lax.Precision.HIGHEST) / weight_total[:, None]
    slide_logits = jnp.dot(pooled, classifier, precision=lax.Precision.HIGHEST)
    total_loss = LOSS_SCALE * jnp.sum(jax.nn.softplus(slide_logits) - label_values * slide_logits)
    return (total_loss, slide_logits)

def normalize(grad):
    return (grad / jnp.sqrt(jnp.mean(grad * grad) + 1e-06)).astype(jnp.bfloat16)

def forward_block(tile_block, w_reduce, w_expand):
    reduced = jax.nn.relu(jnp.dot(tile_block, w_reduce, preferred_element_type=jnp.float32)).astype(jnp.bfloat16)
    preact = tile_block.astype(jnp.float32) + jnp.dot(reduced, w_expand, preferred_element_type=jnp.float32)
    return (reduced, preact)

def reference(features_in, w_reduce, w_expand, att_value, att_gate, att_vector, classifier, tile_slide, labels):
    blocks = TILES // TILE_DEV
    tile_blocks = features_in.reshape(blocks, TILE_DEV * POS, D)

    def features_of(tile_block):
        reduced, preact = forward_block(tile_block, w_reduce, w_expand)
        return lax.optimization_barrier(jnp.mean(jax.nn.relu(preact).reshape(TILE_DEV, POS, D), axis=1)).astype(jnp.bfloat16)
    tile_features = lax.map(features_of, tile_blocks).reshape(TILES, D)
    member = (tile_slide[:, 0][:, None] == jnp.arange(SLIDES, dtype=jnp.int32)[None, :]).astype(jnp.float32)
    label_values = labels.astype(jnp.float32)
    pool_fn = partial(pool_slides, att_value=att_value, att_gate=att_gate, att_vector=att_vector, classifier=classifier, member=member, label_values=label_values)
    total_loss, pool_vjp, slide_logits = jax.vjp(pool_fn, tile_features.astype(jnp.float32), has_aux=True)
    feature_grad = pool_vjp(jnp.ones_like(total_loss))[0].astype(jnp.bfloat16)
    grad_blocks = feature_grad.reshape(blocks, TILE_DEV, D)

    def accumulate(grad_carry, pieces):
        tile_block, grad_rows = pieces
        reduced, preact = forward_block(tile_block, w_reduce, w_expand)
        scaled = (grad_rows.astype(jnp.float32) / POS)[:, None, :]
        pre_grad = jnp.where(preact.reshape(TILE_DEV, POS, D) > 0, scaled, 0.0).astype(jnp.bfloat16).reshape(TILE_DEV * POS, D)
        expand_grad = lax.dot_general(reduced, pre_grad, (((0,), (0,)), ((), ())), preferred_element_type=jnp.float32)
        back_proj = lax.dot_general(pre_grad, w_expand, (((1,), (1,)), ((), ())), preferred_element_type=jnp.float32)
        reduced_grad = jnp.where(reduced > 0, back_proj, 0.0).astype(jnp.bfloat16)
        reduce_grad = lax.dot_general(tile_block, reduced_grad, (((0,), (0,)), ((), ())), preferred_element_type=jnp.float32)
        return ((grad_carry[0] + reduce_grad, grad_carry[1] + expand_grad), None)
    start = (jnp.zeros((D, MID), jnp.float32), jnp.zeros((MID, D), jnp.float32))
    (reduce_grad, expand_grad), _ = lax.scan(accumulate, start, (tile_blocks, grad_blocks))
    return (normalize(reduce_grad), normalize(expand_grad), slide_logits, total_loss)
```

```python
import functools

import jax
import jax.numpy as jnp
from jax import lax
from jax.experimental import pallas as pl
from jax.experimental.pallas import tpu as pltpu
from jax.sharding import PartitionSpec as P

LOSS_SCALE = 1024.0
MESH = pl.DeviceIdType.MESH
F32, BF16 = jnp.float32, jnp.bfloat16
TILES, POS, D, MID, ATT = 32, 49, 2048, 512, 1024
ROWS = TILES * POS
PADDED = 1664
BLOCK = 224
BLOCKS = ROWS // BLOCK
E_PARTS = ((0, 384), (384, 384), (768, 256))
R_PARTS = ((0, 768), (768, 768), (1536, 512))
E_ORDERS = ((0, 1, 2), (1, 2, 0), (2, 0, 1))
R_ORDERS = ((1, 2, 0), (2, 0, 1), (0, 1, 2))
NT = (((1,), (1,)), ((), ()))


class Place:
    def __init__(self):
        self.tile, self.slide = lax.axis_index("tile"), lax.axis_index("slide")
        self.core = lax.rem(self.slide, 2)
        self.at = (lax.div(self.slide, 2), lax.rem(self.tile, 4), lax.div(self.tile, 4))
        self.twin = (self.tile, self.slide + 1 - 2 * self.core)

    def ahead(self, axis, step):
        return lax.rem(self.at[axis] + step, 4)

    def partner(self, axis, step):
        x, y, z = (self.ahead(a, step) if a == axis else self.at[a] for a in range(3))
        return (z * 4 + y, x * 2 + self.core)


class Sems:
    def __init__(self, send, recv):
        self.send, self.recv, self.used = send, recv, 0

    def copy(self, src, dst, device):
        i = self.used
        self.used += 1
        made = pltpu.make_async_remote_copy(
            src_ref=src,
            dst_ref=dst,
            send_sem=self.send.at[i],
            recv_sem=self.recv.at[i],
            device_id=device,
            device_id_type=MESH,
        )
        made.start()
        return made


class Part:
    def __init__(self, place, sems, order, shard, out_shard, quarter, near, far, bufs, local_sem):
        self.place, self.sems, self.order = place, sems, order
        self.shard, self.out_shard, self.quarter = shard, out_shard, quarter
        self.mine, self.theirs, self.got = near
        self.local_sem = local_sem
        self.recv_a, self.sum_a, self.recv_b, self.all_c, self.final, self.full_a = bufs
        self.sent = []

    def send_twin(self):
        self.twin_copy = self.sems.copy(self.theirs, self.got, self.place.twin)
        self.sent.append(self.twin_copy)

    def send_a(self):
        self.twin_copy.wait_recv()
        self.mine[...] = (self.mine[...].astype(F32) + self.got[...].astype(F32)).astype(BF16)
        axis = self.order[0]
        self.a = [
            self.sems.copy(
                self.shard(self.place.ahead(axis, step)),
                self.recv_a.at[step - 1],
                self.place.partner(axis, step),
            )
            for step in (1, 2, 3)
        ]
        self.sent += self.a

    def send_b(self):
        total = self.shard(self.place.at[self.order[0]])[...].astype(F32)
        for i, copy in enumerate(self.a):
            copy.wait_recv()
            total = total + self.recv_a[i].astype(F32)
        self.sum_a[...] = total.astype(BF16)
        axis, rows = self.order[1], self.quarter
        self.b = [
            self.sems.copy(
                self.sum_a.at[pl.ds(pl.multiple_of(self.place.ahead(axis, step) * rows, rows), rows)],
                self.recv_b.at[step - 1],
                self.place.partner(axis, step),
            )
            for step in (1, 2, 3)
        ]
        self.sent += self.b

    def send_c(self):
        rows = self.quarter
        own = pl.ds(pl.multiple_of(self.place.at[self.order[1]] * rows, rows), rows)
        total = self.sum_a[own].astype(F32)
        for i, copy in enumerate(self.b):
            copy.wait_recv()
            total = total + self.recv_b[i].astype(F32)
        axis = self.order[2]
        slot = self.all_c.at[self.place.at[axis]]
        slot[...] = total.astype(BF16)
        self.c = [self.sems.copy(slot, slot, self.place.partner(axis, step)) for step in (1, 2, 3)]
        self.sent += self.c

    def gather_b(self):
        for copy in self.c:
            copy.wait_recv()
        total = self.all_c[0].astype(F32)
        for i in (1, 2, 3):
            total = total + self.all_c[i].astype(F32)
        total = total.astype(BF16)
        self.final[...] = total
        axis, rows = self.order[1], self.quarter
        own = pl.ds(pl.multiple_of(self.place.at[axis] * rows, rows), rows)
        self.full_a[own] = total
        self.gb = [
            self.sems.copy(self.final, self.full_a.at[own], self.place.partner(axis, step))
            for step in (1, 2, 3)
        ]
        self.sent += self.gb

    def gather_a(self):
        for copy in self.gb:
            copy.wait_recv()
        axis = self.order[0]
        target = self.out_shard(self.place.at[axis])
        self.local = pltpu.make_async_copy(self.full_a, target, self.local_sem)
        self.local.start()
        self.ga = [
            self.sems.copy(self.full_a, target, self.place.partner(axis, step)) for step in (1, 2, 3)
        ]
        self.forward = [self.sems.copy(self.full_a, target, self.place.twin)]
        self.sent += self.ga

    def hand_on(self):
        axis = self.order[0]
        for step, copy in zip((1, 2, 3), self.ga):
            copy.wait_recv()
            block = self.out_shard(self.place.ahead(axis, 4 - step))
            self.forward.append(self.sems.copy(block, block, self.place.twin))

    def finish(self):
        for copy in self.forward:
            copy.wait_recv()
        for copy in self.forward + self.sent:
            copy.wait_send()
        self.local.wait()


def part_scratch(shard_rows, width):
    quarter = shard_rows // 4
    shapes = [(3, shard_rows, width), (shard_rows, width), (3, quarter, width), (4, quarter, width)]
    shapes += [(quarter, width), (shard_rows, width)]
    return [pltpu.VMEM(shape, BF16) for shape in shapes]


STAT_STEPS = 1 + 3 + 3 + 3
PART_COPIES = 1 + 3 * 5 + 4
COPIES = STAT_STEPS + 6 * PART_COPIES


def body(
    x_hbm, wr_hbm, we_hbm, av_hbm, ag_hbm, vec_ref, cls_ref, slide_ref, label_ref,
    ge_ref, gr_ref, stat_ref,
    xv, wr, we, av, ag, red, mask, xt, redt, rg, feat, score_part,
    send_e, acc_e, got_e, send_r, acc_r, got_r, stat0, stat1, stat2, stat3,
    x_sem, w_sem, send_sem, recv_sem, local_sem, *part_bufs,
):
    place = Place()
    sems = Sems(send_sem, recv_sem)
    core = place.core

    barrier = pltpu.get_barrier_semaphore()
    partners = [place.twin] + [place.partner(axis, step) for axis in range(3) for step in (1, 2, 3)]
    for device in partners:
        pl.semaphore_signal(barrier, inc=1, device_id=device, device_id_type=MESH)

    def x_copy(i):
        rows = pl.ds(pl.multiple_of(i * BLOCK, BLOCK), BLOCK)
        return pltpu.make_async_copy(x_hbm.at[rows], xv.at[rows], x_sem.at[i])

    weights = ((wr_hbm, wr), (we_hbm, we), (av_hbm, av), (ag_hbm, ag))
    w_copies = [pltpu.make_async_copy(a, b, w_sem.at[i]) for i, (a, b) in enumerate(weights)]
    w_copies[0].start()
    x_copy(0).start()
    w_copies[1].start()
    for i in range(1, BLOCKS):
        x_copy(i).start()
    w_copies[2].start()
    w_copies[3].start()

    tail = PADDED - ROWS
    xv[ROWS:] = jnp.zeros((tail, D), BF16)
    red[ROWS:] = jnp.zeros((tail, MID), BF16)
    mask[ROWS:] = jnp.zeros((tail, D), BF16)
    rg[:, ROWS:] = jnp.zeros((2, tail, MID // 2), BF16)
    feat[...] = jnp.zeros(feat.shape, F32)

    w_copies[0].wait()
    w_copies[1].wait()

    def forward(i, carry):
        rows = pl.ds(pl.multiple_of(i * BLOCK, BLOCK), BLOCK)
        x_copy(i).wait()
        block = jnp.maximum(jnp.dot(xv[rows], wr[...], preferred_element_type=F32), 0.0).astype(BF16)
        red[rows] = block
        for at in range(0, D, 512):
            cols = slice(at, at + 512)
            pre = xv[rows, cols].astype(F32) + jnp.dot(block, we[:, cols], preferred_element_type=F32)
            mask[rows, cols] = jnp.where(pre > 0, 1.0, 0.0).astype(BF16)
            act = jnp.maximum(pre, 0.0).reshape(BLOCK // TILES, TILES, 512)
            feat[:, cols] += jnp.sum(act, axis=0)
        return carry

    lax.fori_loop(0, BLOCKS, forward, 0)

    features = (feat[...] / POS).astype(BF16)
    w_copies[2].wait()
    value = jnp.tanh(jnp.dot(features, av[...], preferred_element_type=F32))
    w_copies[3].wait()
    gate = jax.nn.sigmoid(jnp.dot(features, ag[...], preferred_element_type=F32))
    vector, classes = vec_ref[...], cls_ref[...]
    scores = jnp.sum(value * gate * vector, axis=1, keepdims=True)
    weight = jnp.exp(scores)
    along = jnp.sum(features.astype(F32) * classes, axis=1, keepdims=True)

    lane = lax.broadcasted_iota(jnp.int32, (TILES, 128), 1)
    square = (TILES, TILES)
    diagonal = lax.broadcasted_iota(jnp.int32, square, 0) == lax.broadcasted_iota(jnp.int32, square, 1)
    named = jnp.where(diagonal, jnp.broadcast_to(slide_ref[...].astype(F32), square), 0.0)
    named = jnp.sum(named, axis=1, keepdims=True)
    member = jnp.where(named == lane.astype(F32), 1.0, 0.0)
    lane_row = lax.broadcasted_iota(jnp.int32, (1, 128), 1)
    label_row = jnp.where(lane_row == place.slide, label_ref[0].astype(F32), 0.0)
    weight_row = jnp.sum(member * weight, axis=0, keepdims=True)
    along_row = jnp.sum(member * (weight * (along * 2.0**-8)), axis=0, keepdims=True)

    slots = (stat0, stat1, stat2, stat3)
    spots = (core,) + place.at

    def stat_send(step):
        slot = slots[step].at[spots[step]]
        if step == 0:
            return [sems.copy(slot, slot, place.twin)]
        return [sems.copy(slot, slot, place.partner(step - 1, ahead)) for ahead in (1, 2, 3)]

    def stat_sum(step, copies):
        for copy in copies:
            copy.wait_recv()
        total = slots[step][0]
        for i in range(1, slots[step].shape[0]):
            total = total + slots[step][i]
        return total

    def transpose_x(first, last):
        def turn(i, carry):
            cols = pl.ds(pl.multiple_of(i * 256, 256), 256)
            xt[cols, :] = xv[:, cols].T
            return carry

        lax.fori_loop(first, last, turn, 0)

    def put(step, rows):
        slots[step][spots[step]] = rows

    stat_rows = jnp.concatenate([weight_row, along_row, label_row, jnp.zeros((5, 128), F32)], axis=0)
    put(0, stat_rows)
    pl.semaphore_wait(barrier, len(partners))
    stat_copies = []
    copies = stat_send(0)
    stat_copies += copies

    def split(cot):
        high = cot.astype(BF16)
        return jnp.concatenate([high, (cot - high.astype(F32)).astype(BF16)], axis=0)

    value_cot = split(vector * (1.0 - value * value) * gate)
    gate_cot = split(vector * value * gate * (1.0 - gate))
    for at in range(0, D, 512):
        cols = slice(at, at + 512)
        both = lax.dot_general(value_cot, av[cols, :], NT, preferred_element_type=F32)
        both = both + lax.dot_general(gate_cot, ag[cols, :], NT, preferred_element_type=F32)
        score_part[:, cols] = both[:TILES] + both[TILES:]

    put(1, stat_sum(0, copies))
    copies = stat_send(1)
    stat_copies += copies
    transpose_x(0, 4)
    put(2, stat_sum(1, copies))
    copies = stat_send(2)
    stat_copies += copies
    transpose_x(4, 8)
    put(3, stat_sum(2, copies))
    copies = stat_send(3)
    stat_copies += copies
    redt[...] = red[...].T
    totals = stat_sum(3, copies)
    for copy in stat_copies:
        copy.wait_send()

    live = lane_row < 8
    weight_total = jnp.where(live, totals[0:1], 1.0)
    logits = jnp.where(live, totals[1:2], 0.0) / weight_total * 2.0**8
    labels = totals[2:3] / 16.0
    losses = jnp.maximum(logits, 0.0) + jnp.log1p(jnp.exp(-jnp.abs(logits))) - labels * logits
    loss = LOSS_SCALE * jnp.sum(jnp.where(live, losses, 0.0))
    own_logit = jnp.sum(jnp.where(lane_row == place.slide, logits, 0.0))
    stat_ref[0:1] = jnp.full((1, 128), own_logit, F32)
    stat_ref[1:2] = jnp.full((1, 128), loss, F32)
    stat_ref[2:8] = jnp.zeros((6, 128), F32)
    slope = LOSS_SCALE * (jax.nn.sigmoid(logits) - labels)

    def of_tile(row):
        return jnp.sum(member * row, axis=1, keepdims=True)

    share = weight / of_tile(weight_total)
    pull = share * of_tile(slope)
    score_grad = pull * (along - of_tile(logits))
    grad = (pull * classes + score_grad * score_part[...]).astype(BF16)
    scaled = (grad.astype(F32) / POS).astype(BF16)

    def mask_rows(i, carry):
        rows = pl.ds(pl.multiple_of(i * BLOCK, BLOCK), BLOCK)
        spread = jnp.broadcast_to(scaled[None], (BLOCK // TILES, TILES, D)).reshape(BLOCK, D)
        mask[rows] = mask[rows] * spread
        return carry

    lax.fori_loop(0, BLOCKS, mask_rows, 0)

    def expand_cols(half, store):
        def chunk(i, carry):
            cols = pl.ds(pl.multiple_of(half * (D // 2) + i * 256, 256), 256)
            out = jnp.dot(redt[...], mask[:, cols], preferred_element_type=F32).astype(BF16)
            store[:, pl.ds(pl.multiple_of(i * 256, 256), 256)] = out
            return carry

        lax.fori_loop(0, D // 2 // 256, chunk, 0)

    e_parts, r_parts = [], []
    for p, (first, width) in enumerate(E_PARTS):
        cols = pl.ds(first, width)

        def e_shard(k, cols=cols):
            return acc_e.at[pl.ds(pl.multiple_of(k * 128, 128), 128), cols]

        def e_out(k, first=first, width=width):
            rows = pl.ds(pl.multiple_of(k * 128, 128), 128)
            return ge_ref.at[rows, pl.ds(pl.multiple_of(core * (D // 2) + first, 128), width)]

        near = (acc_e.at[:, cols], send_e.at[:, cols], got_e.at[:, cols])
        e_parts.append(
            Part(place, sems, E_ORDERS[p], e_shard, e_out, 32, near, None,
                 part_bufs[6 * p : 6 * p + 6], local_sem.at[p])
        )
    for p, (first, height) in enumerate(R_PARTS):
        rows = pl.ds(first, height)
        quarter = height // 4

        def r_shard(k, first=first, quarter=quarter):
            return acc_r.at[pl.ds(pl.multiple_of(first + k * quarter, 64), quarter)]

        def r_out(k, first=first, quarter=quarter):
            at = pl.ds(pl.multiple_of(first + k * quarter, 64), quarter)
            return gr_ref.at[at, pl.ds(pl.multiple_of(core * 256, 256), 256)]

        near = (acc_r.at[rows], send_r.at[rows], got_r.at[rows])
        r_parts.append(
            Part(place, sems, R_ORDERS[p], r_shard, r_out, quarter // 4, near, None,
                 part_bufs[6 * (3 + p) : 6 * (3 + p) + 6], local_sem.at[3 + p])
        )

    expand_cols(1 - core, send_e)
    for part in e_parts:
        part.send_twin()
    expand_cols(core, acc_e)
    for part in e_parts:
        part.send_a()

    def back(i, carry):
        rows = pl.ds(pl.multiple_of(i * BLOCK, BLOCK), BLOCK)
        proj = lax.dot_general(mask[rows], we[...], NT, preferred_element_type=F32)
        proj = jnp.where(red[rows] > 0, proj, 0.0).astype(BF16)
        rg[0, rows] = proj[:, : MID // 2]
        rg[1, rows] = proj[:, MID // 2 :]
        return carry

    lax.fori_loop(0, BLOCKS, back, 0)

    def reduce_rows(part, half, store):
        first, height = part

        def chunk(i, carry):
            rows = pl.ds(pl.multiple_of(first + i * 256, 256), 256)
            store[rows] = jnp.dot(xt[rows], rg[half], preferred_element_type=F32).astype(BF16)
            return carry

        lax.fori_loop(0, height // 256, chunk, 0)

    for p in range(3):
        reduce_rows(R_PARTS[p], 1 - core, send_r)
        r_parts[p].send_twin()
        e_parts[p].send_b()
        reduce_rows(R_PARTS[p], core, acc_r)
        r_parts[p].send_a()
        e_parts[p].send_c()
    for part in e_parts:
        part.gather_b()
    for part in r_parts:
        part.send_b()
    for part in e_parts:
        part.gather_a()
    for part in r_parts:
        part.send_c()
    for part in r_parts:
        part.gather_b()
    for part in e_parts:
        part.hand_on()
    for part in r_parts:
        part.gather_a()
    for part in r_parts:
        part.hand_on()
    for part in e_parts + r_parts:
        part.finish()


def pooled_gradients(x, wr, we, av, ag, vector, classes, slides, labels):
    any_space = pl.BlockSpec(memory_space=pl.ANY)
    vmem = pl.BlockSpec(memory_space=pltpu.VMEM)
    smem = pl.BlockSpec(memory_space=pltpu.SMEM)
    scratch = [
        pltpu.VMEM((PADDED, D), BF16),
        pltpu.VMEM((D, MID), BF16),
        pltpu.VMEM((MID, D), BF16),
        pltpu.VMEM((D, ATT), BF16),
        pltpu.VMEM((D, ATT), BF16),
        pltpu.VMEM((PADDED, MID), BF16),
        pltpu.VMEM((PADDED, D), BF16),
        pltpu.VMEM((D, PADDED), BF16),
        pltpu.VMEM((MID, PADDED), BF16),
        pltpu.VMEM((2, PADDED, MID // 2), BF16),
        pltpu.VMEM((TILES, D), F32),
        pltpu.VMEM((TILES, D), F32),
    ]
    scratch += [pltpu.VMEM((MID, D // 2), BF16)] * 3
    scratch += [pltpu.VMEM((D, MID // 2), BF16)] * 3
    scratch += [pltpu.VMEM((n, 8, 128), F32) for n in (2, 4, 4, 4)]
    scratch += [
        pltpu.SemaphoreType.DMA((BLOCKS,)),
        pltpu.SemaphoreType.DMA((4,)),
        pltpu.SemaphoreType.DMA((COPIES,)),
        pltpu.SemaphoreType.DMA((COPIES,)),
        pltpu.SemaphoreType.DMA((6,)),
    ]
    for _, width in E_PARTS:
        scratch += part_scratch(128, width)
    for _, height in R_PARTS:
        scratch += part_scratch(height // 4, MID // 2)
    return pl.pallas_call(
        body,
        name="pooled_gradients",
        out_shape=(
            jax.ShapeDtypeStruct((MID, D), BF16),
            jax.ShapeDtypeStruct((D, MID), BF16),
            jax.ShapeDtypeStruct((8, 128), F32),
        ),
        in_specs=[any_space] * 5 + [vmem] * 3 + [smem],
        out_specs=(any_space, any_space, vmem),
        scratch_shapes=scratch,
        cost_estimate=pl.CostEstimate(flops=17_000_000_000, bytes_accessed=24_000_000, transcendentals=70_000),
        compiler_params=pltpu.CompilerParams(
            collective_id=0, has_side_effects=True, vmem_limit_bytes=60 * 2**20
        ),
    )(x, wr, we, av, ag, vector, classes, slides, labels)


def normalize_body(ge_hbm, gr_hbm, stat_ref, ue_hbm, ur_hbm, logit_ref, loss_ref, ge, gr, ue, ur, in_sem, out_sem):
    logit_ref[0] = stat_ref[0, 0]
    loss_ref[0] = stat_ref[1, 0]
    pieces = 4
    jobs = ((ge_hbm, ge, ue, ue_hbm), (gr_hbm, gr, ur, ur_hbm))
    copies = []
    for m, (hbm, vmem, _, _) in enumerate(jobs):
        rows = vmem.shape[0] // pieces
        for i in range(pieces):
            at = pl.ds(i * rows, rows)
            copy = pltpu.make_async_copy(hbm.at[at], vmem.at[at], in_sem.at[m * pieces + i])
            copy.start()
            copies.append(copy)
    outs = []
    for m, (_, vmem, scaled, hbm) in enumerate(jobs):
        rows = vmem.shape[0] // pieces
        width = vmem.shape[1]
        total = jnp.zeros((8, width), F32)
        for i in range(pieces):
            copies[m * pieces + i].wait()
            values = vmem[i * rows : (i + 1) * rows].astype(F32)
            total = total + jnp.sum((values * values).reshape(rows // 8, 8, width), axis=0)
        mean = jnp.sum(total) / (D * MID)
        scale = 1.0 / jnp.sqrt(jnp.full((1, width), mean + 1e-06, F32))
        for i in range(pieces):
            at = slice(i * rows, (i + 1) * rows)
            scaled[at] = (vmem[at].astype(F32) * scale).astype(BF16)
            copy = pltpu.make_async_copy(scaled.at[pl.ds(i * rows, rows)], hbm.at[pl.ds(i * rows, rows)], out_sem.at[m * pieces + i])
            copy.start()
            outs.append(copy)
    for copy in outs:
        copy.wait()


def normalize(ge, gr, stat):
    any_space = pl.BlockSpec(memory_space=pl.ANY)
    smem = pl.BlockSpec(memory_space=pltpu.SMEM)
    return pl.pallas_call(
        normalize_body,
        name="normalize",
        out_shape=(
            jax.ShapeDtypeStruct((MID, D), BF16),
            jax.ShapeDtypeStruct((D, MID), BF16),
            jax.ShapeDtypeStruct((1,), F32),
            jax.ShapeDtypeStruct((1,), F32),
        ),
        in_specs=[any_space, any_space, smem],
        out_specs=(any_space, any_space, smem, smem),
        scratch_shapes=[
            pltpu.VMEM((MID, D), BF16),
            pltpu.VMEM((D, MID), BF16),
            pltpu.VMEM((MID, D), BF16),
            pltpu.VMEM((D, MID), BF16),
            pltpu.SemaphoreType.DMA((8,)),
            pltpu.SemaphoreType.DMA((8,)),
        ],
        compiler_params=pltpu.CompilerParams(vmem_limit_bytes=60 * 2**20),
    )(ge, gr, stat)


def shards(
    features_in, w_reduce, w_expand, att_value, att_gate, att_vector, classifier, tile_slide, labels
):
    rows = features_in.transpose(1, 0, 2).reshape(ROWS, D)
    ge, gr, stat = pooled_gradients(
        rows, w_reduce, w_expand, att_value, att_gate,
        att_vector.reshape(1, ATT), classifier.reshape(1, D), tile_slide.reshape(1, TILES), labels,
    )
    update_expand, update_reduce, logit, loss = normalize(ge, gr, stat)
    return (update_reduce, update_expand, logit, loss.reshape(()))


def solution(mesh):
    placed = (
        P(("tile", "slide"), None, None),
        P(),
        P(),
        P(),
        P(),
        P(),
        P(),
        P(("tile", "slide"), None),
        P("slide"),
    )
    return jax.shard_map(
        shards, mesh=mesh, in_specs=placed, out_specs=(P(), P(), P("slide"), P()), check_vma=False
    )
```

```python
import functools

import jax
import jax.numpy as jnp
from jax import lax
from jax.experimental import pallas as pl
from jax.experimental.pallas import tpu as pltpu
from jax.sharding import PartitionSpec as P

LOSS_SCALE = 1024.0
MESH = pl.DeviceIdType.MESH
F32, BF16 = jnp.float32, jnp.bfloat16
TILES, POS, D, MID, ATT = 32, 49, 2048, 512, 1024
ROWS = TILES * POS
PADDED = 1664
BLOCK = 224
BLOCKS = ROWS // BLOCK
X_BLOCKS = ((0, 416), (416, 384), (800, 384), (1184, 384))
CHUNK = 256
HALF = D // 2
E_COUNT, E_SHARD, E_SHIFT = 4, 128, 0
R_COUNT, R_SHARD, R_SHIFT = 8, 64, 1
TWIN, LINE_A, LINE_B, LINE_C, BACK_B, BACK_A, HAND = range(7)
NT = (((1,), (1,)), ((), ()))


class Place:
    def __init__(self):
        self.tile, self.slide = lax.axis_index("tile"), lax.axis_index("slide")
        self.core = lax.rem(self.slide, 2)
        self.coords = (lax.div(self.slide, 2), lax.rem(self.tile, 4), lax.div(self.tile, 4))
        self.twin = (self.tile, self.slide + 1 - 2 * self.core)

    def picks(self, axis):
        return ((2 - axis) * (1 - axis) // 2, axis * (2 - axis), axis * (axis - 1) // 2)

    def at(self, axis):
        return sum(pick * c for pick, c in zip(self.picks(axis), self.coords))

    def ahead(self, axis, step):
        return lax.rem(self.at(axis) + step, 4)

    def partner(self, axis, step):
        x, y, z = (lax.rem(c + pick * step, 4) for pick, c in zip(self.picks(axis), self.coords))
        return (z * 4 + y, x * 2 + self.core)


def start_copy(src, dst, send_sem, recv_sem, device):
    pltpu.make_async_remote_copy(
        src_ref=src, dst_ref=dst, send_sem=send_sem, recv_sem=recv_sem, device_id=device, device_id_type=MESH
    ).start()


def wait_bytes(like, sem):
    pltpu.make_async_copy(like, like, sem).wait()


class Sum:
    def __init__(self, place, shift, shard, out_shard, near, bufs, recv, send, local):
        self.place, self.shift, self.shard_rows, self.out_shard = place, shift, shard, out_shard
        self.theirs, self.mine, self.got = near
        self.recv_a, self.sum_a, self.recv_b, self.all_c, self.final, self.full_a = bufs
        self.recv, self.send, self.local = recv, send, local

    def axis(self, p, turn):
        return lax.rem(p + self.shift + turn, 3)

    def shard(self, p, k):
        rows = self.shard_rows
        return pl.ds(pl.multiple_of((p * 4 + k) * rows, rows), rows)

    def quarter(self, k):
        rows = self.shard_rows // 4
        return pl.ds(pl.multiple_of(k * rows, rows), rows)

    def part(self, p):
        rows = 4 * self.shard_rows
        return pl.ds(pl.multiple_of(p * rows, rows), rows)

    def to_line(self, p, stage, axis, src, dst):
        for step in (1, 2, 3):
            start_copy(src(step), dst(step), self.send.at[p], self.recv.at[p, stage], self.place.partner(axis, step))

    def send_twin(self, p):
        rows = self.part(p)
        start_copy(self.theirs.at[rows], self.got.at[rows], self.send.at[p], self.recv.at[p, TWIN], self.place.twin)

    def send_a(self, p):
        rows = self.part(p)
        wait_bytes(self.got.at[rows], self.recv.at[p, TWIN])
        self.mine[rows] = (self.mine[rows].astype(F32) + self.got[rows].astype(F32)).astype(BF16)
        wait_bytes(self.theirs.at[rows], self.send.at[p])
        axis = self.axis(p, 0)
        self.to_line(
            p, LINE_A, axis,
            lambda step: self.mine.at[self.shard(p, self.place.ahead(axis, step))],
            lambda step: self.recv_a.at[p, step - 1],
        )

    def send_b(self, p):
        wait_bytes(self.recv_a.at[p], self.recv.at[p, LINE_A])
        total = self.mine[self.shard(p, self.place.at(self.axis(p, 0)))].astype(F32)
        for i in range(3):
            total = total + self.recv_a[p, i].astype(F32)
        self.sum_a[p] = total.astype(BF16)
        wait_bytes(self.recv_a.at[p], self.send.at[p])
        axis = self.axis(p, 1)
        self.to_line(
            p, LINE_B, axis,
            lambda step: self.sum_a.at[p, self.quarter(self.place.ahead(axis, step))],
            lambda step: self.recv_b.at[p, step - 1],
        )

    def send_c(self, p):
        wait_bytes(self.recv_b.at[p], self.recv.at[p, LINE_B])
        total = self.sum_a[p, self.quarter(self.place.at(self.axis(p, 1)))].astype(F32)
        for i in range(3):
            total = total + self.recv_b[p, i].astype(F32)
        axis = self.axis(p, 2)
        slot = self.all_c.at[p, self.place.at(axis)]
        slot[...] = total.astype(BF16)
        wait_bytes(self.recv_b.at[p], self.send.at[p])
        self.to_line(p, LINE_C, axis, lambda step: slot, lambda step: slot)

    def gather_b(self, p):
        wait_bytes(self.recv_b.at[p], self.recv.at[p, LINE_C])
        total = self.all_c[p, 0].astype(F32)
        for i in (1, 2, 3):
            total = total + self.all_c[p, i].astype(F32)
        total = total.astype(BF16)
        self.final[p] = total
        axis = self.axis(p, 1)
        own = self.quarter(self.place.at(axis))
        self.full_a[p, own] = total
        wait_bytes(self.recv_b.at[p], self.send.at[p])
        self.to_line(p, BACK_B, axis, lambda step: self.final.at[p], lambda step: self.full_a.at[p, own])

    def gather_a(self, p):
        wait_bytes(self.recv_b.at[p], self.recv.at[p, BACK_B])
        wait_bytes(self.recv_b.at[p], self.send.at[p])
        axis = self.axis(p, 0)
        target = self.out_shard(p, self.place.at(axis))
        source = self.full_a.at[p]
        self.to_line(p, BACK_A, axis, lambda step: source, lambda step: target)
        start_copy(source, target, self.send.at[p], self.recv.at[p, HAND], self.place.twin)
        pltpu.make_async_copy(source, target, self.local).start()

    def hand_on(self, p):
        wait_bytes(self.recv_a.at[p], self.recv.at[p, BACK_A])
        wait_bytes(self.mine.at[self.part(p)], self.send.at[p])
        axis = self.axis(p, 0)
        for step in (1, 2, 3):
            block = self.out_shard(p, self.place.ahead(axis, step))
            start_copy(block, block, self.send.at[p], self.recv.at[p, HAND], self.place.twin)

    def finish(self, p):
        wait_bytes(self.mine.at[self.part(p)], self.recv.at[p, HAND])
        wait_bytes(self.recv_a.at[p], self.send.at[p])


def part_scratch(count, rows, width):
    quarter = rows // 4
    shapes = [(3, rows), (rows,), (3, quarter), (4, quarter), (quarter,), (rows,)]
    return [pltpu.VMEM((count,) + shape + (width,), BF16) for shape in shapes]


def body(
    x_hbm, wr_hbm, we_hbm, av_hbm, ag_hbm, vec_ref, cls_ref, slide_ref, label_ref,
    ge_ref, gr_ref, stat_ref,
    xv, wr, we, av, ag, red, mask, xt, redt, rg, feat, score_part,
    send_e, acc_e, got_e, send_r, acc_r, got_r, stat0, stat1, stat2, stat3,
    x_sem, w_sem, stat_recv, stat_send_sem, recv_e, recv_r, done_e, done_r, local_sem, *part_bufs,
):
    place = Place()
    core = place.core

    barrier = pltpu.get_barrier_semaphore()
    partners = [place.twin] + [place.partner(axis, step) for axis in range(3) for step in (1, 2, 3)]
    for device in partners:
        pl.semaphore_signal(barrier, inc=1, device_id=device, device_id_type=MESH)

    x_copies = [
        pltpu.make_async_copy(x_hbm.at[pl.ds(first, rows)], xv.at[pl.ds(first, rows)], x_sem.at[i])
        for i, (first, rows) in enumerate(X_BLOCKS)
    ]
    weights = ((wr_hbm, wr), (we_hbm, we), (av_hbm, av), (ag_hbm, ag))
    w_copies = [pltpu.make_async_copy(a, b, w_sem.at[i]) for i, (a, b) in enumerate(weights)]
    w_copies[0].start()
    x_copies[0].start()
    x_copies[1].start()

    tail = PADDED - ROWS
    xv[ROWS:] = jnp.zeros((tail, D), BF16)
    red[ROWS:] = jnp.zeros((tail, MID), BF16)
    mask[ROWS:] = jnp.zeros((tail, D), BF16)
    rg[:, ROWS:] = jnp.zeros((2, tail, MID // 2), BF16)

    w_copies[0].wait()
    for i, (first, height) in enumerate(X_BLOCKS):
        x_copies[i].wait()
        if i == 0:
            x_copies[2].start()
            x_copies[3].start()
            w_copies[1].start()
        if i == 1:
            w_copies[2].start()
            w_copies[3].start()
        rows = slice(first, first + height)
        block = jnp.dot(xv[rows], wr[...], preferred_element_type=F32)
        red[rows] = jnp.maximum(block, 0.0).astype(BF16)

    w_copies[1].wait()

    def forward(i, carry):
        cols = pl.ds(pl.multiple_of(i * CHUNK, CHUNK), CHUNK)
        pre = jnp.dot(red[:ROWS], we[:, cols], preferred_element_type=F32)
        pre = xv[:ROWS, cols].astype(F32) + pre
        mask[:ROWS, cols] = jnp.where(pre > 0, 1.0, 0.0).astype(BF16)
        feat[:, cols] = jnp.sum(jnp.maximum(pre, 0.0).reshape(POS, TILES, CHUNK), axis=0)
        return carry

    lax.fori_loop(0, D // CHUNK, forward, 0)

    features = (feat[...] / POS).astype(BF16)
    w_copies[2].wait()
    value = jnp.tanh(jnp.dot(features, av[...], preferred_element_type=F32))
    w_copies[3].wait()
    gate = jax.nn.sigmoid(jnp.dot(features, ag[...], preferred_element_type=F32))
    vector, classes = vec_ref[...], cls_ref[...]
    scores = jnp.sum(value * gate * vector, axis=1, keepdims=True)
    weight = jnp.exp(scores)
    along = jnp.sum(features.astype(F32) * classes, axis=1, keepdims=True)

    lane = lax.broadcasted_iota(jnp.int32, (TILES, 128), 1)
    square = (TILES, TILES)
    diagonal = lax.broadcasted_iota(jnp.int32, square, 0) == lax.broadcasted_iota(jnp.int32, square, 1)
    named = jnp.where(diagonal, jnp.broadcast_to(slide_ref[...].astype(F32), square), 0.0)
    named = jnp.sum(named, axis=1, keepdims=True)
    member = jnp.where(named == lane.astype(F32), 1.0, 0.0)
    lane_row = lax.broadcasted_iota(jnp.int32, (1, 128), 1)
    label_row = jnp.where(lane_row == place.slide, label_ref[0].astype(F32), 0.0)
    weight_row = jnp.sum(member * weight, axis=0, keepdims=True)
    along_row = jnp.sum(member * (weight * (along * 2.0**-8)), axis=0, keepdims=True)

    slots = (stat0, stat1, stat2, stat3)
    spots = (core,) + place.coords

    def stat_send(step):
        slot = slots[step].at[spots[step]]
        devices = [place.twin] if step == 0 else [place.partner(step - 1, ahead) for ahead in (1, 2, 3)]
        for device in devices:
            start_copy(slot, slot, stat_send_sem.at[step], stat_recv.at[step], device)

    def stat_sum(step):
        others = slots[step].at[pl.ds(0, slots[step].shape[0] - 1)]
        wait_bytes(others, stat_recv.at[step])
        wait_bytes(others, stat_send_sem.at[step])
        total = slots[step][0]
        for i in range(1, slots[step].shape[0]):
            total = total + slots[step][i]
        return total

    def transpose_x(first, last):
        def turn(i, carry):
            cols = pl.ds(pl.multiple_of(i * 256, 256), 256)
            xt[cols, :] = xv[:, cols].T
            return carry

        lax.fori_loop(first, last, turn, 0)

    def put(step, rows):
        slots[step][spots[step]] = rows

    stat_rows = jnp.concatenate([weight_row, along_row, label_row, jnp.zeros((5, 128), F32)], axis=0)
    put(0, stat_rows)
    pl.semaphore_wait(barrier, len(partners))
    stat_send(0)

    def split(cot):
        high = cot.astype(BF16)
        return jnp.concatenate([high, (cot - high.astype(F32)).astype(BF16)], axis=0)

    value_cot = split(vector * (1.0 - value * value) * gate)
    gate_cot = split(vector * value * gate * (1.0 - gate))

    def score_cols(i, carry):
        cols = pl.ds(pl.multiple_of(i * 512, 512), 512)
        both = lax.dot_general(value_cot, av[cols, :], NT, preferred_element_type=F32)
        both = both + lax.dot_general(gate_cot, ag[cols, :], NT, preferred_element_type=F32)
        score_part[:, cols] = both[:TILES] + both[TILES:]
        return carry

    lax.fori_loop(0, D // 512, score_cols, 0)
    put(1, stat_sum(0))
    stat_send(1)
    transpose_x(0, 4)
    put(2, stat_sum(1))
    stat_send(2)
    transpose_x(4, 8)
    put(3, stat_sum(2))
    stat_send(3)
    redt[...] = red[...].T
    totals = stat_sum(3)

    live = lane_row < 8
    weight_total = jnp.where(live, totals[0:1], 1.0)
    logits = jnp.where(live, totals[1:2], 0.0) / weight_total * 2.0**8
    labels = totals[2:3] / 16.0
    losses = jnp.maximum(logits, 0.0) + jnp.log1p(jnp.exp(-jnp.abs(logits))) - labels * logits
    loss = LOSS_SCALE * jnp.sum(jnp.where(live, losses, 0.0))
    own_logit = jnp.sum(jnp.where(lane_row == place.slide, logits, 0.0))
    stat_ref[0:1] = jnp.full((1, 128), own_logit, F32)
    stat_ref[1:2] = jnp.full((1, 128), loss, F32)
    stat_ref[2:8] = jnp.zeros((6, 128), F32)
    slope = LOSS_SCALE * (jax.nn.sigmoid(logits) - labels)

    def of_tile(row):
        return jnp.sum(member * row, axis=1, keepdims=True)

    share = weight / of_tile(weight_total)
    pull = share * of_tile(slope)
    score_grad = pull * (along - of_tile(logits))
    grad = (pull * classes + score_grad * score_part[...]).astype(BF16)
    scaled = (grad.astype(F32) / POS).astype(BF16)

    def mask_rows(i, carry):
        rows = pl.ds(pl.multiple_of(i * BLOCK, BLOCK), BLOCK)
        spread = jnp.broadcast_to(scaled[None], (BLOCK // TILES, TILES, D)).reshape(BLOCK, D)
        mask[rows] = mask[rows] * spread
        return carry

    lax.fori_loop(0, BLOCKS, mask_rows, 0)

    def e_out(p, k):
        rows = pl.ds(pl.multiple_of(k * E_SHARD, E_SHARD), E_SHARD)
        return ge_ref.at[rows, pl.ds(pl.multiple_of(core * HALF + p * CHUNK, CHUNK), CHUNK)]

    def r_out(p, k):
        rows = pl.ds(pl.multiple_of((p * 4 + k) * R_SHARD, R_SHARD), R_SHARD)
        return gr_ref.at[rows, pl.ds(pl.multiple_of(core * CHUNK, CHUNK), CHUNK)]

    e_sum = Sum(place, E_SHIFT, E_SHARD, e_out, (send_e, acc_e, got_e), part_bufs[:6], recv_e, done_e, local_sem.at[0])
    r_sum = Sum(place, R_SHIFT, R_SHARD, r_out, (send_r, acc_r, got_r), part_bufs[6:], recv_r, done_r, local_sem.at[1])

    def pair(step, k):
        step(2 * k)
        step(2 * k + 1)

    def expand(i, carry):
        for turn, store in ((1, send_e), (0, acc_e)):
            half = lax.rem(core + turn, 2)
            cols = pl.ds(pl.multiple_of(half * HALF + i * CHUNK, CHUNK), CHUNK)
            out = jnp.dot(redt[...], mask[:, cols], preferred_element_type=F32)
            store[e_sum.part(i)] = out.astype(BF16)
        e_sum.send_twin(i)
        pl.when(i > 0)(lambda: e_sum.send_a(i - 1))
        return carry

    lax.fori_loop(0, E_COUNT, expand, 0)

    def back(i, carry):
        rows = pl.ds(pl.multiple_of(i * (ROWS // 2), 16), ROWS // 2)
        proj = lax.dot_general(mask[rows], we[...], NT, preferred_element_type=F32)
        proj = jnp.where(red[rows] > 0, proj, 0.0).astype(BF16)
        rg[0, rows] = proj[:, :CHUNK]
        rg[1, rows] = proj[:, CHUNK:]
        pl.when(i == 0)(lambda: e_sum.send_a(E_COUNT - 1))
        return carry

    lax.fori_loop(0, 2, back, 0)

    def reduce(i, carry):
        rows = pl.ds(pl.multiple_of(i * 512, 512), 512)
        for turn, store in ((1, send_r), (0, acc_r)):
            half = lax.rem(core + turn, 2)
            store[rows] = jnp.dot(xt[rows], rg[half], preferred_element_type=F32).astype(BF16)
        pair(r_sum.send_twin, i)
        pl.when(i > 0)(lambda: pair(r_sum.send_a, i - 1))
        e_sum.send_b(i)
        return carry

    lax.fori_loop(0, 4, reduce, 0)
    pair(r_sum.send_a, 3)

    plan = (
        (0, e_sum.send_c, 1),
        (1, r_sum.send_b, 2),
        (2, e_sum.gather_b, 1),
        (4, r_sum.send_c, 2),
        (5, e_sum.gather_a, 1),
        (7, r_sum.gather_b, 2),
        (10, e_sum.hand_on, 1),
        (10, r_sum.gather_a, 2),
        (13, r_sum.hand_on, 2),
        (14, e_sum.finish, 1),
        (15, r_sum.finish, 2),
    )

    def tail_step(t, carry):
        for first, step, width in plan:
            k = t - first

            @pl.when((k >= 0) & (k < 4))
            def _(k=k, step=step, width=width):
                if width == 2:
                    pair(step, k)
                else:
                    step(k)

        return carry

    lax.fori_loop(0, plan[-1][0] + 4, tail_step, 0)
    wait_bytes(acc_e.at[e_sum.part(0)], local_sem.at[0])
    wait_bytes(acc_e.at[e_sum.part(0)], local_sem.at[1])


def pooled_gradients(x, wr, we, av, ag, vector, classes, slides, labels):
    any_space = pl.BlockSpec(memory_space=pl.ANY)
    vmem = pl.BlockSpec(memory_space=pltpu.VMEM)
    smem = pl.BlockSpec(memory_space=pltpu.SMEM)
    scratch = [
        pltpu.VMEM((PADDED, D), BF16),
        pltpu.VMEM((D, MID), BF16),
        pltpu.VMEM((MID, D), BF16),
        pltpu.VMEM((D, ATT), BF16),
        pltpu.VMEM((D, ATT), BF16),
        pltpu.VMEM((PADDED, MID), BF16),
        pltpu.VMEM((PADDED, D), BF16),
        pltpu.VMEM((D, PADDED), BF16),
        pltpu.VMEM((MID, PADDED), BF16),
        pltpu.VMEM((2, PADDED, MID // 2), BF16),
        pltpu.VMEM((TILES, D), F32),
        pltpu.VMEM((TILES, D), F32),
    ]
    scratch += [pltpu.VMEM((E_COUNT * MID, CHUNK), BF16)] * 3
    scratch += [pltpu.VMEM((D, MID // 2), BF16)] * 3
    scratch += [pltpu.VMEM((n, 8, 128), F32) for n in (2, 4, 4, 4)]
    scratch += [
        pltpu.SemaphoreType.DMA((len(X_BLOCKS),)),
        pltpu.SemaphoreType.DMA((4,)),
        pltpu.SemaphoreType.DMA((4,)),
        pltpu.SemaphoreType.DMA((4,)),
        pltpu.SemaphoreType.DMA((E_COUNT, 7)),
        pltpu.SemaphoreType.DMA((R_COUNT, 7)),
        pltpu.SemaphoreType.DMA((E_COUNT,)),
        pltpu.SemaphoreType.DMA((R_COUNT,)),
        pltpu.SemaphoreType.DMA((2,)),
    ]
    scratch += part_scratch(E_COUNT, E_SHARD, CHUNK)
    scratch += part_scratch(R_COUNT, R_SHARD, CHUNK)
    return pl.pallas_call(
        body,
        name="pooled_gradients",
        out_shape=(
            jax.ShapeDtypeStruct((MID, D), BF16),
            jax.ShapeDtypeStruct((D, MID), BF16),
            jax.ShapeDtypeStruct((8, 128), F32),
        ),
        in_specs=[any_space] * 5 + [vmem] * 3 + [smem],
        out_specs=(any_space, any_space, vmem),
        scratch_shapes=scratch,
        cost_estimate=pl.CostEstimate(flops=17_000_000_000, bytes_accessed=24_000_000, transcendentals=70_000),
        compiler_params=pltpu.CompilerParams(
            collective_id=0, has_side_effects=True, vmem_limit_bytes=60 * 2**20
        ),
    )(x, wr, we, av, ag, vector, classes, slides, labels)


def normalize_body(ge_hbm, gr_hbm, stat_ref, ue_hbm, ur_hbm, logit_ref, loss_ref, ge, gr, ue, ur, in_sem, out_sem):
    logit_ref[0] = stat_ref[0, 0]
    loss_ref[0] = stat_ref[1, 0]
    pieces = 4
    jobs = ((ge_hbm, ge, ue, ue_hbm), (gr_hbm, gr, ur, ur_hbm))
    copies = []
    for m, (hbm, vmem, _, _) in enumerate(jobs):
        rows = vmem.shape[0] // pieces
        for i in range(pieces):
            at = pl.ds(i * rows, rows)
            copy = pltpu.make_async_copy(hbm.at[at], vmem.at[at], in_sem.at[m * pieces + i])
            copy.start()
            copies.append(copy)
    outs = []
    for m, (_, vmem, scaled, hbm) in enumerate(jobs):
        rows = vmem.shape[0] // pieces
        width = vmem.shape[1]
        total = jnp.zeros((8, width), F32)
        for i in range(pieces):
            copies[m * pieces + i].wait()
            values = vmem[i * rows : (i + 1) * rows].astype(F32)
            total = total + jnp.sum((values * values).reshape(rows // 8, 8, width), axis=0)
        mean = jnp.sum(total) / (D * MID)
        scale = 1.0 / jnp.sqrt(jnp.full((1, width), mean + 1e-06, F32))
        for i in range(pieces):
            at = slice(i * rows, (i + 1) * rows)
            scaled[at] = (vmem[at].astype(F32) * scale).astype(BF16)
            copy = pltpu.make_async_copy(scaled.at[pl.ds(i * rows, rows)], hbm.at[pl.ds(i * rows, rows)], out_sem.at[m * pieces + i])
            copy.start()
            outs.append(copy)
    for copy in outs:
        copy.wait()


def normalize(ge, gr, stat):
    any_space = pl.BlockSpec(memory_space=pl.ANY)
    smem = pl.BlockSpec(memory_space=pltpu.SMEM)
    return pl.pallas_call(
        normalize_body,
        name="normalize",
        out_shape=(
            jax.ShapeDtypeStruct((MID, D), BF16),
            jax.ShapeDtypeStruct((D, MID), BF16),
            jax.ShapeDtypeStruct((1,), F32),
            jax.ShapeDtypeStruct((1,), F32),
        ),
        in_specs=[any_space, any_space, smem],
        out_specs=(any_space, any_space, smem, smem),
        scratch_shapes=[
            pltpu.VMEM((MID, D), BF16),
            pltpu.VMEM((D, MID), BF16),
            pltpu.VMEM((MID, D), BF16),
            pltpu.VMEM((D, MID), BF16),
            pltpu.SemaphoreType.DMA((8,)),
            pltpu.SemaphoreType.DMA((8,)),
        ],
        compiler_params=pltpu.CompilerParams(vmem_limit_bytes=60 * 2**20),
    )(ge, gr, stat)


def shards(
    features_in, w_reduce, w_expand, att_value, att_gate, att_vector, classifier, tile_slide, labels
):
    rows = features_in.transpose(1, 0, 2).reshape(ROWS, D)
    ge, gr, stat = pooled_gradients(
        rows, w_reduce, w_expand, att_value, att_gate,
        att_vector.reshape(1, ATT), classifier.reshape(1, D), tile_slide.reshape(1, TILES), labels,
    )
    update_expand, update_reduce, logit, loss = normalize(ge, gr, stat)
    return (update_reduce, update_expand, logit, loss.reshape(()))


def solution(mesh):
    placed = (
        P(("tile", "slide"), None, None),
        P(),
        P(),
        P(),
        P(),
        P(),
        P(),
        P(("tile", "slide"), None),
        P("slide"),
    )
    return jax.shard_map(
        shards, mesh=mesh, in_specs=placed, out_specs=(P(), P(), P("slide"), P()), check_vma=False
    )
```

```python
import functools

import jax
import jax.numpy as jnp
from jax import lax
from jax.experimental import pallas as pl
from jax.experimental.pallas import tpu as pltpu
from jax.sharding import PartitionSpec as P

LOSS_SCALE = 1024.0
MESH = pl.DeviceIdType.MESH
F32, BF16 = jnp.float32, jnp.bfloat16
TILES, POS, D, MID, ATT = 32, 49, 2048, 512, 1024
ROWS = TILES * POS
PADDED = 1664
BLOCK = 224
BLOCKS = ROWS // BLOCK
X_BLOCKS = ((0, 416), (416, 384), (800, 384), (1184, 384))
CHUNK = 256
HALF = D // 2
E_COUNT, E_SHARD, E_SHIFT, E_WIDTH = 8, 128, 0, 128
R_COUNT, R_SHARD, R_SHIFT = 8, 64, 1
TWIN, LINE_A, LINE_B, LINE_C, BACK_B, BACK_A, HAND = range(7)
NT = (((1,), (1,)), ((), ()))


class Place:
    def __init__(self):
        self.tile, self.slide = lax.axis_index("tile"), lax.axis_index("slide")
        self.core = lax.rem(self.slide, 2)
        self.at = (lax.div(self.slide, 2), lax.rem(self.tile, 4), lax.div(self.tile, 4))
        self.twin = (self.tile, self.slide + 1 - 2 * self.core)
        self.ahead = [[lax.rem(c + step, 4) for step in range(4)] for c in self.at]

    def partner(self, axis, step):
        x, y, z = (self.ahead[a][step] if a == axis else c for a, c in enumerate(self.at))
        return (z * 4 + y, x * 2 + self.core)


def start_copy(src, dst, send_sem, recv_sem, device):
    pltpu.make_async_remote_copy(
        src_ref=src, dst_ref=dst, send_sem=send_sem, recv_sem=recv_sem, device_id=device, device_id_type=MESH
    ).start()


def wait_bytes(like, sem):
    pltpu.make_async_copy(like, like, sem).wait()


class Sum:
    def __init__(self, place, shift, shard, out_part, near, bufs, recv, send):
        self.place, self.shift, self.shard_rows, self.out_part = place, shift, shard, out_part
        self.theirs, self.mine, self.got = near
        self.recv_a, self.sum_a, self.recv_b, self.all_c = bufs
        self.recv, self.send = recv, send

    def axis(self, p, turn):
        return (p + self.shift + turn) % 3

    def shard(self, p, k):
        rows = self.shard_rows
        return pl.ds(pl.multiple_of((p * 4 + k) * rows, rows), rows)

    def quarter(self, k):
        rows = self.shard_rows // 4
        return pl.ds(pl.multiple_of(k * rows, rows), rows)

    def part(self, p):
        rows = 4 * self.shard_rows
        return pl.ds(p * rows, rows)

    def whole(self, k):
        rows = 8 * self.shard_rows
        return pl.ds(k * rows, rows)

    def shards(self, k):
        return self.recv_a.at[pl.ds(2 * k, 2)]

    def quarters(self, k):
        return self.recv_b.at[pl.ds(2 * k, 2)]

    def to_line(self, p, stage, axis, src, dst):
        k = p // 2
        for step in (1, 2, 3):
            start_copy(src(step), dst(step), self.send.at[k], self.recv.at[k, stage], self.place.partner(axis, step))

    def to_twin(self, k, stage, src, dst):
        start_copy(src, dst, self.send.at[k], self.recv.at[k, stage], self.place.twin)

    def send_twin(self, k):
        rows = self.whole(k)
        self.to_twin(k, TWIN, self.theirs.at[rows], self.got.at[rows])

    def send_a(self, k):
        rows = self.whole(k)
        wait_bytes(self.got.at[rows], self.recv.at[k, TWIN])
        self.mine[rows] = (self.mine[rows].astype(F32) + self.got[rows].astype(F32)).astype(BF16)
        wait_bytes(self.theirs.at[rows], self.send.at[k])
        for p in (2 * k, 2 * k + 1):
            axis = self.axis(p, 0)
            self.to_line(
                p, LINE_A, axis,
                lambda step: self.mine.at[self.shard(p, self.place.ahead[axis][step])],
                lambda step: self.recv_a.at[p, step - 1],
            )

    def send_b(self, k):
        wait_bytes(self.shards(k), self.recv.at[k, LINE_A])
        wait_bytes(self.shards(k), self.send.at[k])
        for p in (2 * k, 2 * k + 1):
            total = self.mine[self.shard(p, self.place.at[self.axis(p, 0)])].astype(F32)
            for i in range(3):
                total = total + self.recv_a[p, i].astype(F32)
            self.sum_a[p] = total.astype(BF16)
            axis = self.axis(p, 1)
            self.to_line(
                p, LINE_B, axis,
                lambda step: self.sum_a.at[p, self.quarter(self.place.ahead[axis][step])],
                lambda step: self.recv_b.at[p, step - 1],
            )

    def send_c(self, k):
        wait_bytes(self.quarters(k), self.recv.at[k, LINE_B])
        wait_bytes(self.quarters(k), self.send.at[k])
        for p in (2 * k, 2 * k + 1):
            total = self.sum_a[p, self.quarter(self.place.at[self.axis(p, 1)])].astype(F32)
            for i in range(3):
                total = total + self.recv_b[p, i].astype(F32)
            axis = self.axis(p, 2)
            slot = self.all_c.at[p, self.place.at[axis]]
            slot[...] = total.astype(BF16)
            self.to_line(p, LINE_C, axis, lambda step: slot, lambda step: slot)

    def gather_b(self, k):
        wait_bytes(self.quarters(k), self.recv.at[k, LINE_C])
        wait_bytes(self.quarters(k), self.send.at[k])
        for p in (2 * k, 2 * k + 1):
            total = self.all_c[p, 0].astype(F32)
            for i in (1, 2, 3):
                total = total + self.all_c[p, i].astype(F32)
            axis = self.axis(p, 1)
            rows = self.shard_rows // 4
            own = self.out_part(p, self.place.at[self.axis(p, 0)] * 4 + self.place.at[axis], rows)
            own[...] = total.astype(BF16)
            self.to_line(p, BACK_B, axis, lambda step: own, lambda step: own)

    def gather_a(self, k):
        wait_bytes(self.quarters(k), self.recv.at[k, BACK_B])
        wait_bytes(self.quarters(k), self.send.at[k])
        for p in (2 * k, 2 * k + 1):
            axis = self.axis(p, 0)
            own = self.out_part(p, self.place.at[axis], self.shard_rows)
            self.to_line(p, BACK_A, axis, lambda step: own, lambda step: own)
        for p in (2 * k, 2 * k + 1):
            own = self.out_part(p, self.place.at[self.axis(p, 0)], self.shard_rows)
            self.to_twin(k, HAND, own, own)

    def hand_on(self, k):
        wait_bytes(self.shards(k), self.recv.at[k, BACK_A])
        wait_bytes(self.mine.at[self.whole(k)], self.send.at[k])
        for p in (2 * k, 2 * k + 1):
            for step in (1, 2, 3):
                block = self.out_part(p, self.place.ahead[self.axis(p, 0)][step], self.shard_rows)
                self.to_twin(k, HAND, block, block)

    def finish(self, k):
        wait_bytes(self.mine.at[self.whole(k)], self.recv.at[k, HAND])
        wait_bytes(self.shards(k), self.send.at[k])


def inverse_rms(ref):
    height, width = ref.shape
    total = jnp.zeros((8, width), F32)
    for i in range(0, height, 64):
        values = ref[i : i + 64].astype(F32)
        total = total + jnp.sum((values * values).reshape(8, 8, width), axis=0)
    mean = jnp.sum(total) / (D * MID)
    return 1.0 / jnp.sqrt(jnp.full((1, width), mean + 1e-06, F32))


def part_scratch(count, rows, width):
    quarter = rows // 4
    shapes = [(3, rows), (rows,), (3, quarter), (4, quarter)]
    return [pltpu.VMEM((count,) + shape + (width,), BF16) for shape in shapes]


def body(
    x_hbm, wr_hbm, we_hbm, av_hbm, ag_hbm, vec_ref, cls_ref, slide_ref, label_ref,
    ge_ref, gr_ref, stat_ref,
    xv, wr, we, av, ag, red, mask, xt, redt, rg, feat, score_part,
    send_e, acc_e, got_e, send_r, acc_r, got_r, stat0, stat1, stat2, stat3,
    x_sem, w_sem, stat_recv, stat_send_sem, recv_e, recv_r, done_e, done_r, *part_bufs,
):
    place = Place()
    core = place.core

    barrier = pltpu.get_barrier_semaphore()
    partners = [place.twin] + [place.partner(axis, step) for axis in range(3) for step in (1, 2, 3)]
    for device in partners:
        pl.semaphore_signal(barrier, inc=1, device_id=device, device_id_type=MESH)

    x_copies = [
        pltpu.make_async_copy(x_hbm.at[pl.ds(first, rows)], xv.at[pl.ds(first, rows)], x_sem.at[i])
        for i, (first, rows) in enumerate(X_BLOCKS)
    ]
    weights = ((wr_hbm, wr), (we_hbm, we), (av_hbm, av), (ag_hbm, ag))
    w_copies = [pltpu.make_async_copy(a, b, w_sem.at[i]) for i, (a, b) in enumerate(weights)]
    w_copies[0].start()
    x_copies[0].start()

    tail = PADDED - ROWS
    xv[ROWS:] = jnp.zeros((tail, D), BF16)
    red[ROWS:] = jnp.zeros((tail, MID), BF16)
    mask[ROWS:] = jnp.zeros((tail, D), BF16)
    rg[:, ROWS:] = jnp.zeros((2, tail, MID // 2), BF16)

    w_copies[0].wait()
    x_copies[1].start()
    for i, (first, height) in enumerate(X_BLOCKS):
        x_copies[i].wait()
        if i == 0:
            x_copies[2].start()
            x_copies[3].start()
            w_copies[1].start()
        if i == 1:
            w_copies[2].start()
            w_copies[3].start()
        rows = slice(first, first + height)
        block = jnp.dot(xv[rows], wr[...], preferred_element_type=F32)
        red[rows] = jnp.maximum(block, 0.0).astype(BF16)

    w_copies[1].wait()

    def forward(i, carry):
        cols = pl.ds(pl.multiple_of(i * CHUNK, CHUNK), CHUNK)
        pre = jnp.dot(red[:ROWS], we[:, cols], preferred_element_type=F32)
        pre = xv[:ROWS, cols].astype(F32) + pre
        mask[:ROWS, cols] = jnp.where(pre > 0, 1.0, 0.0).astype(BF16)
        feat[:, cols] = jnp.sum(jnp.maximum(pre, 0.0).reshape(POS, TILES, CHUNK), axis=0)
        return carry

    lax.fori_loop(0, D // CHUNK, forward, 0)

    features = (feat[...] / POS).astype(BF16)
    w_copies[2].wait()
    value = jnp.tanh(jnp.dot(features, av[...], preferred_element_type=F32))
    w_copies[3].wait()
    gate = jax.nn.sigmoid(jnp.dot(features, ag[...], preferred_element_type=F32))
    vector, classes = vec_ref[...], cls_ref[...]
    scores = jnp.sum(value * gate * vector, axis=1, keepdims=True)
    weight = jnp.exp(scores)
    along = jnp.sum(features.astype(F32) * classes, axis=1, keepdims=True)

    lane = lax.broadcasted_iota(jnp.int32, (TILES, 128), 1)
    square = (TILES, TILES)
    diagonal = lax.broadcasted_iota(jnp.int32, square, 0) == lax.broadcasted_iota(jnp.int32, square, 1)
    named = jnp.where(diagonal, jnp.broadcast_to(slide_ref[...].astype(F32), square), 0.0)
    named = jnp.sum(named, axis=1, keepdims=True)
    member = jnp.where(named == lane.astype(F32), 1.0, 0.0)
    lane_row = lax.broadcasted_iota(jnp.int32, (1, 128), 1)
    label_row = jnp.where(lane_row == place.slide, label_ref[0].astype(F32), 0.0)
    weight_row = jnp.sum(member * weight, axis=0, keepdims=True)
    along_row = jnp.sum(member * (weight * (along * 2.0**-8)), axis=0, keepdims=True)

    slots = (stat0, stat1, stat2, stat3)
    spots = (core,) + place.at

    def stat_send(step):
        slot = slots[step].at[spots[step]]
        devices = [place.twin] if step == 0 else [place.partner(step - 1, ahead) for ahead in (1, 2, 3)]
        for device in devices:
            start_copy(slot, slot, stat_send_sem.at[step], stat_recv.at[step], device)

    def stat_sum(step):
        others = slots[step].at[pl.ds(0, slots[step].shape[0] - 1)]
        wait_bytes(others, stat_recv.at[step])
        wait_bytes(others, stat_send_sem.at[step])
        total = slots[step][0]
        for i in range(1, slots[step].shape[0]):
            total = total + slots[step][i]
        return total

    def transpose_x(first, last):
        def turn(i, carry):
            cols = pl.ds(pl.multiple_of(i * 256, 256), 256)
            xt[cols, :] = xv[:, cols].T
            return carry

        lax.fori_loop(first, last, turn, 0)

    def put(step, rows):
        slots[step][spots[step]] = rows

    stat_rows = jnp.concatenate([weight_row, along_row, label_row, jnp.zeros((5, 128), F32)], axis=0)
    put(0, stat_rows)
    pl.semaphore_wait(barrier, len(partners))
    stat_send(0)

    def split(cot):
        high = cot.astype(BF16)
        return jnp.concatenate([high, (cot - high.astype(F32)).astype(BF16)], axis=0)

    value_cot = split(vector * (1.0 - value * value) * gate)
    gate_cot = split(vector * value * gate * (1.0 - gate))

    def score_cols(i, carry):
        cols = pl.ds(pl.multiple_of(i * 512, 512), 512)
        both = lax.dot_general(value_cot, av[cols, :], NT, preferred_element_type=F32)
        both = both + lax.dot_general(gate_cot, ag[cols, :], NT, preferred_element_type=F32)
        score_part[:, cols] = both[:TILES] + both[TILES:]
        return carry

    lax.fori_loop(0, D // 512, score_cols, 0)
    put(1, stat_sum(0))
    stat_send(1)
    transpose_x(0, 4)
    put(2, stat_sum(1))
    stat_send(2)
    transpose_x(4, 8)
    put(3, stat_sum(2))
    stat_send(3)
    redt[...] = red[...].T
    totals = stat_sum(3)

    live = lane_row < 8
    weight_total = jnp.where(live, totals[0:1], 1.0)
    logits = jnp.where(live, totals[1:2], 0.0) / weight_total * 2.0**8
    labels = totals[2:3] / 16.0
    losses = jnp.maximum(logits, 0.0) + jnp.log1p(jnp.exp(-jnp.abs(logits))) - labels * logits
    loss = LOSS_SCALE * jnp.sum(jnp.where(live, losses, 0.0))
    own_logit = jnp.sum(jnp.where(lane_row == place.slide, logits, 0.0))
    stat_ref[0:1] = jnp.full((1, 128), own_logit, F32)
    stat_ref[1:2] = jnp.full((1, 128), loss, F32)
    stat_ref[2:8] = jnp.zeros((6, 128), F32)
    slope = LOSS_SCALE * (jax.nn.sigmoid(logits) - labels)

    def of_tile(row):
        return jnp.sum(member * row, axis=1, keepdims=True)

    share = weight / of_tile(weight_total)
    pull = share * of_tile(slope)
    score_grad = pull * (along - of_tile(logits))
    grad = (pull * classes + score_grad * score_part[...]).astype(BF16)
    scaled = (grad.astype(F32) / POS).astype(BF16)

    def mask_rows(i, carry):
        rows = pl.ds(pl.multiple_of(i * BLOCK, BLOCK), BLOCK)
        spread = jnp.broadcast_to(scaled[None], (BLOCK // TILES, TILES, D)).reshape(BLOCK, D)
        mask[rows] = mask[rows] * spread
        return carry

    lax.fori_loop(0, BLOCKS, mask_rows, 0)

    def e_out(p, k, rows):
        at = pl.ds(pl.multiple_of(k * rows, rows), rows)
        return ge_ref.at[at, pl.ds(pl.multiple_of(core * HALF + p * E_WIDTH, E_WIDTH), E_WIDTH)]

    def r_out(p, k, rows):
        at = pl.ds(pl.multiple_of(p * 4 * R_SHARD + k * rows, rows), rows)
        return gr_ref.at[at, pl.ds(pl.multiple_of(core * CHUNK, CHUNK), CHUNK)]

    e_sum = Sum(place, E_SHIFT, E_SHARD, e_out, (send_e, acc_e, got_e), part_bufs[:4], recv_e, done_e)
    r_sum = Sum(place, R_SHIFT, R_SHARD, r_out, (send_r, acc_r, got_r), part_bufs[4:], recv_r, done_r)

    def expand(i):
        for turn, store in ((1, send_e), (0, acc_e)):
            half = lax.rem(core + turn, 2)
            cols = pl.ds(pl.multiple_of(half * HALF + i * CHUNK, CHUNK), CHUNK)
            out = jnp.dot(redt[...], mask[:, cols], preferred_element_type=F32).astype(BF16)
            store[e_sum.part(2 * i)] = out[:, :E_WIDTH]
            store[e_sum.part(2 * i + 1)] = out[:, E_WIDTH:]

    def back(i):
        rows = slice(i * (ROWS // 2), (i + 1) * (ROWS // 2))
        proj = lax.dot_general(mask[rows], we[...], NT, preferred_element_type=F32)
        proj = jnp.where(red[rows] > 0, proj, 0.0).astype(BF16)
        rg[0, rows] = proj[:, :CHUNK]
        rg[1, rows] = proj[:, CHUNK:]

    def reduce(i):
        rows = slice(i * 512, (i + 1) * 512)
        for turn, store in ((1, send_r), (0, acc_r)):
            half = lax.rem(core + turn, 2)
            store[rows] = jnp.dot(xt[rows], rg[half], preferred_element_type=F32).astype(BF16)

    for i in range(4):
        expand(i)
        e_sum.send_twin(i)
        if i > 0:
            e_sum.send_a(i - 1)
    back(0)
    e_sum.send_a(3)
    back(1)
    for i in range(4):
        e_sum.send_b(i)
        reduce(i)
        r_sum.send_twin(i)
        if i > 0:
            r_sum.send_a(i - 1)
        if i > 1:
            e_sum.send_c(i - 2)
    r_sum.send_a(3)

    starts = (
        (0.4, r_sum.send_b),
        (4.0, r_sum.send_c),
        (7.6, r_sum.gather_b),
        (11.2, r_sum.gather_a),
        (16.0, r_sum.hand_on),
        (-2.5, e_sum.send_c),
        (1.0, e_sum.gather_b),
        (4.6, e_sum.gather_a),
        (11.4, e_sum.hand_on),
    )
    events = [(at + 1.4 * k, n, k) for n, (at, _) in enumerate(starts) for k in range(4)]
    for at, n, k in sorted(events):
        step = starts[n][1]
        if step != e_sum.send_c or k > 1:
            step(k)
        if step == r_sum.hand_on and k == 0:
            for i in range(4):
                e_sum.finish(i)
            scale = inverse_rms(ge_ref)
            for i in range(0, MID, 64):
                ge_ref[i : i + 64] = (ge_ref[i : i + 64].astype(F32) * scale).astype(BF16)
    for k in range(4):
        r_sum.finish(k)


def pooled_gradients(x, wr, we, av, ag, vector, classes, slides, labels):
    any_space = pl.BlockSpec(memory_space=pl.ANY)
    vmem = pl.BlockSpec(memory_space=pltpu.VMEM)
    smem = pl.BlockSpec(memory_space=pltpu.SMEM)
    scratch = [
        pltpu.VMEM((PADDED, D), BF16),
        pltpu.VMEM((D, MID), BF16),
        pltpu.VMEM((MID, D), BF16),
        pltpu.VMEM((D, ATT), BF16),
        pltpu.VMEM((D, ATT), BF16),
        pltpu.VMEM((PADDED, MID), BF16),
        pltpu.VMEM((PADDED, D), BF16),
        pltpu.VMEM((D, PADDED), BF16),
        pltpu.VMEM((MID, PADDED), BF16),
        pltpu.VMEM((2, PADDED, MID // 2), BF16),
        pltpu.VMEM((TILES, D), F32),
        pltpu.VMEM((TILES, D), F32),
    ]
    scratch += [pltpu.VMEM((E_COUNT * MID, E_WIDTH), BF16)] * 3
    scratch += [pltpu.VMEM((D, MID // 2), BF16)] * 3
    scratch += [pltpu.VMEM((n, 8, 128), F32) for n in (2, 4, 4, 4)]
    scratch += [
        pltpu.SemaphoreType.DMA((len(X_BLOCKS),)),
        pltpu.SemaphoreType.DMA((4,)),
        pltpu.SemaphoreType.DMA((4,)),
        pltpu.SemaphoreType.DMA((4,)),
        pltpu.SemaphoreType.DMA((4, 7)),
        pltpu.SemaphoreType.DMA((4, 7)),
        pltpu.SemaphoreType.DMA((4,)),
        pltpu.SemaphoreType.DMA((4,)),
    ]
    scratch += part_scratch(E_COUNT, E_SHARD, E_WIDTH)
    scratch += part_scratch(R_COUNT, R_SHARD, CHUNK)
    return pl.pallas_call(
        body,
        name="pooled_gradients",
        out_shape=(
            pltpu.VMEM((MID, D), BF16),
            pltpu.VMEM((D, MID), BF16),
            pltpu.VMEM((8, 128), F32),
        ),
        in_specs=[any_space] * 5 + [vmem] * 3 + [smem],
        out_specs=(vmem, vmem, vmem),
        scratch_shapes=scratch,
        cost_estimate=pl.CostEstimate(flops=17_000_000_000, bytes_accessed=24_000_000, transcendentals=70_000),
        compiler_params=pltpu.CompilerParams(
            collective_id=0, has_side_effects=True, vmem_limit_bytes=54 * 2**20
        ),
    )(x, wr, we, av, ag, vector, classes, slides, labels)


def normalize_body(ue_ref, gr_ref, stat_ref, ue_hbm, ur_hbm, logit_ref, loss_ref, ur, sems):
    whole = pltpu.make_async_copy(ue_ref, ue_hbm, sems.at[0])
    whole.start()
    scale = inverse_rms(gr_ref)
    rows = D // 4
    copies = [whole]
    for i in range(4):
        at = pl.ds(i * rows, rows)
        ur[at] = (gr_ref[at].astype(F32) * scale).astype(BF16)
        copies.append(pltpu.make_async_copy(ur.at[at], ur_hbm.at[at], sems.at[1 + i]))
        copies[-1].start()
    logit_ref[0] = stat_ref[0, 0]
    loss_ref[0] = stat_ref[1, 0]
    for copy in copies:
        copy.wait()


def normalize(ue, gr, stat):
    any_space = pl.BlockSpec(memory_space=pl.ANY)
    vmem = pl.BlockSpec(memory_space=pltpu.VMEM)
    smem = pl.BlockSpec(memory_space=pltpu.SMEM)
    return pl.pallas_call(
        normalize_body,
        name="normalize",
        out_shape=(
            jax.ShapeDtypeStruct((MID, D), BF16),
            jax.ShapeDtypeStruct((D, MID), BF16),
            jax.ShapeDtypeStruct((1,), F32),
            jax.ShapeDtypeStruct((1,), F32),
        ),
        in_specs=[vmem, vmem, vmem],
        out_specs=(any_space, any_space, smem, smem),
        scratch_shapes=[pltpu.VMEM((D, MID), BF16), pltpu.SemaphoreType.DMA((5,))],
        compiler_params=pltpu.CompilerParams(vmem_limit_bytes=16 * 2**20),
    )(ue, gr, stat)


def shards(
    features_in, w_reduce, w_expand, att_value, att_gate, att_vector, classifier, tile_slide, labels
):
    rows = features_in.transpose(1, 0, 2).reshape(ROWS, D)
    ge, gr, stat = pooled_gradients(
        rows, w_reduce, w_expand, att_value, att_gate,
        att_vector.reshape(1, ATT), classifier.reshape(1, D), tile_slide.reshape(1, TILES), labels,
    )
    update_expand, update_reduce, logit, loss = normalize(ge, gr, stat)
    return (update_reduce, update_expand, logit, loss.reshape(()))


def solution(mesh):
    placed = (
        P(("tile", "slide"), None, None),
        P(),
        P(),
        P(),
        P(),
        P(),
        P(),
        P(("tile", "slide"), None),
        P("slide"),
    )
    return jax.shard_map(
        shards, mesh=mesh, in_specs=placed, out_specs=(P(), P(), P("slide"), P()), check_vma=False
    )
```

```python
import functools

import jax
import jax.numpy as jnp
from jax import lax
from jax.experimental import pallas as pl
from jax.experimental.pallas import tpu as pltpu
from jax.sharding import PartitionSpec as P

LOSS_SCALE = 1024.0
MESH = pl.DeviceIdType.MESH
F32, BF16 = jnp.float32, jnp.bfloat16
TILES, POS, D, MID, ATT = 32, 49, 2048, 512, 1024
ROWS = TILES * POS
PADDED = 1664
BLOCK = 224
BLOCKS = ROWS // BLOCK
X_BLOCKS = ((0, 416), (416, 384), (800, 384), (1184, 384))
CHUNK = 256
HALF = D // 2
E_COUNT, E_SHARD, E_SHIFT, E_WIDTH = 8, 128, 0, 128
R_COUNT, R_SHARD, R_SHIFT = 8, 64, 1
TWIN, LINE_A, LINE_B, LINE_C, BACK_B, BACK_A, HAND = range(7)
NT = (((1,), (1,)), ((), ()))
EXPAND_DONE = 16.1


class Place:
    def __init__(self):
        self.tile, self.slide = lax.axis_index("tile"), lax.axis_index("slide")
        self.core = lax.rem(self.slide, 2)
        self.at = (lax.div(self.slide, 2), lax.rem(self.tile, 4), lax.div(self.tile, 4))
        self.twin = (self.tile, self.slide + 1 - 2 * self.core)
        self.ahead = [[lax.rem(c + step, 4) for step in range(4)] for c in self.at]

    def across(self, step):
        tile, slide = self.partner(0, step)
        return (tile, slide + 1 - 2 * self.core)

    def partner(self, axis, step):
        x, y, z = (self.ahead[a][step] if a == axis else c for a, c in enumerate(self.at))
        return (z * 4 + y, x * 2 + self.core)


def start_copy(src, dst, send_sem, recv_sem, device):
    pltpu.make_async_remote_copy(
        src_ref=src, dst_ref=dst, send_sem=send_sem, recv_sem=recv_sem, device_id=device, device_id_type=MESH
    ).start()


def wait_bytes(like, sem):
    pltpu.make_async_copy(like, like, sem).wait()


class Sum:
    def __init__(self, place, shift, shard, out_part, near, bufs, recv, send):
        self.place, self.shift, self.shard_rows, self.out_part = place, shift, shard, out_part
        self.theirs, self.mine, self.got = near
        self.recv_a, self.sum_a, self.recv_b, self.all_c = bufs
        self.recv, self.send = recv, send

    def axis(self, p, turn):
        return (p + self.shift + turn) % 3

    def shard(self, p, k):
        rows = self.shard_rows
        return pl.ds(pl.multiple_of((p * 4 + k) * rows, rows), rows)

    def quarter(self, k):
        rows = self.shard_rows // 4
        return pl.ds(pl.multiple_of(k * rows, rows), rows)

    def part(self, p):
        rows = 4 * self.shard_rows
        return pl.ds(p * rows, rows)

    def whole(self, k):
        rows = 8 * self.shard_rows
        return pl.ds(k * rows, rows)

    def shards(self, k):
        return self.recv_a.at[pl.ds(2 * k, 2)]

    def quarters(self, k):
        return self.recv_b.at[pl.ds(2 * k, 2)]

    def to_line(self, p, stage, axis, src, dst):
        k = p // 2
        for step in (1, 2, 3):
            start_copy(src(step), dst(step), self.send.at[k], self.recv.at[k, stage], self.place.partner(axis, step))

    def to_twin(self, k, stage, src, dst):
        start_copy(src, dst, self.send.at[k], self.recv.at[k, stage], self.place.twin)

    def send_twin(self, k):
        rows = self.whole(k)
        self.to_twin(k, TWIN, self.theirs.at[rows], self.got.at[rows])

    def send_a(self, k):
        rows = self.whole(k)
        wait_bytes(self.got.at[rows], self.recv.at[k, TWIN])
        self.mine[rows] = (self.mine[rows].astype(F32) + self.got[rows].astype(F32)).astype(BF16)
        wait_bytes(self.theirs.at[rows], self.send.at[k])
        for p in (2 * k, 2 * k + 1):
            axis = self.axis(p, 0)
            self.to_line(
                p, LINE_A, axis,
                lambda step: self.mine.at[self.shard(p, self.place.ahead[axis][step])],
                lambda step: self.recv_a.at[p, step - 1],
            )

    def send_b(self, k):
        wait_bytes(self.shards(k), self.recv.at[k, LINE_A])
        wait_bytes(self.shards(k), self.send.at[k])
        for p in (2 * k, 2 * k + 1):
            total = self.mine[self.shard(p, self.place.at[self.axis(p, 0)])].astype(F32)
            for i in range(3):
                total = total + self.recv_a[p, i].astype(F32)
            self.sum_a[p] = total.astype(BF16)
            axis = self.axis(p, 1)
            self.to_line(
                p, LINE_B, axis,
                lambda step: self.sum_a.at[p, self.quarter(self.place.ahead[axis][step])],
                lambda step: self.recv_b.at[p, step - 1],
            )

    def send_c(self, k):
        wait_bytes(self.quarters(k), self.recv.at[k, LINE_B])
        wait_bytes(self.quarters(k), self.send.at[k])
        for p in (2 * k, 2 * k + 1):
            total = self.sum_a[p, self.quarter(self.place.at[self.axis(p, 1)])].astype(F32)
            for i in range(3):
                total = total + self.recv_b[p, i].astype(F32)
            axis = self.axis(p, 2)
            slot = self.all_c.at[p, self.place.at[axis]]
            slot[...] = total.astype(BF16)
            self.to_line(p, LINE_C, axis, lambda step: slot, lambda step: slot)

    def gather_b(self, k):
        wait_bytes(self.quarters(k), self.recv.at[k, LINE_C])
        wait_bytes(self.quarters(k), self.send.at[k])
        for p in (2 * k, 2 * k + 1):
            total = self.all_c[p, 0].astype(F32)
            for i in (1, 2, 3):
                total = total + self.all_c[p, i].astype(F32)
            axis = self.axis(p, 1)
            rows = self.shard_rows // 4
            own = self.out_part(p, self.place.at[self.axis(p, 0)] * 4 + self.place.at[axis], rows)
            own[...] = total.astype(BF16)
            self.to_line(p, BACK_B, axis, lambda step: own, lambda step: own)

    def gather_a(self, k):
        wait_bytes(self.quarters(k), self.recv.at[k, BACK_B])
        wait_bytes(self.quarters(k), self.send.at[k])
        for p in (2 * k, 2 * k + 1):
            axis = self.axis(p, 0)
            own = self.out_part(p, self.place.at[axis], self.shard_rows)
            self.to_line(p, BACK_A, axis, lambda step: own, lambda step: own)
        for p in (2 * k, 2 * k + 1):
            own = self.out_part(p, self.place.at[self.axis(p, 0)], self.shard_rows)
            self.to_twin(k, HAND, own, own)

    def hand_on(self, k):
        wait_bytes(self.shards(k), self.recv.at[k, BACK_A])
        wait_bytes(self.mine.at[self.whole(k)], self.send.at[k])
        for p in (2 * k, 2 * k + 1):
            for step in (1, 2, 3):
                block = self.out_part(p, self.place.ahead[self.axis(p, 0)][step], self.shard_rows)
                self.to_twin(k, HAND, block, block)

    def finish(self, k):
        wait_bytes(self.mine.at[self.whole(k)], self.recv.at[k, HAND])
        wait_bytes(self.shards(k), self.send.at[k])


def inverse_rms(ref):
    height, width = ref.shape
    total = jnp.zeros((8, width), F32)
    for i in range(0, height, 64):
        values = ref[i : i + 64].astype(F32)
        total = total + jnp.sum((values * values).reshape(8, 8, width), axis=0)
    mean = jnp.sum(total) / (D * MID)
    return 1.0 / jnp.sqrt(jnp.full((1, width), mean + 1e-06, F32))


def part_scratch(count, rows, width):
    quarter = rows // 4
    shapes = [(3, rows), (rows,), (3, quarter), (4, quarter)]
    return [pltpu.VMEM((count,) + shape + (width,), BF16) for shape in shapes]


def body(
    x_hbm, wr_hbm, we_hbm, av_hbm, ag_hbm, vec_ref, cls_ref, slide_ref, label_ref,
    ge_ref, gr_ref, stat_ref,
    xv, wr, we, av, ag, red, mask, xt, redt, rg, feat, score_part,
    send_e, acc_e, got_e, send_r, acc_r, got_r, stat0, stat1, stat2,
    x_sem, w_sem, stat_recv, stat_send_sem, recv_e, recv_r, done_e, done_r, *part_bufs,
):
    place = Place()
    core = place.core

    x_copies = [
        pltpu.make_async_copy(x_hbm.at[pl.ds(first, rows)], xv.at[pl.ds(first, rows)], x_sem.at[i])
        for i, (first, rows) in enumerate(X_BLOCKS)
    ]
    weights = ((wr_hbm, wr), (we_hbm, we), (av_hbm, av), (ag_hbm, ag))
    w_copies = [pltpu.make_async_copy(a, b, w_sem.at[i]) for i, (a, b) in enumerate(weights)]
    w_copies[0].start()
    x_copies[0].start()

    barrier = pltpu.get_barrier_semaphore()
    partners = [place.twin] + [place.partner(axis, step) for axis in range(3) for step in (1, 2, 3)]
    partners += [place.across(step) for step in (1, 2, 3)]
    for device in partners:
        pl.semaphore_signal(barrier, inc=1, device_id=device, device_id_type=MESH)

    tail = PADDED - ROWS
    xv[ROWS:] = jnp.zeros((tail, D), BF16)
    red[ROWS:] = jnp.zeros((tail, MID), BF16)
    mask[ROWS:] = jnp.zeros((tail, D), BF16)
    rg[:, ROWS:] = jnp.zeros((2, tail, MID // 2), BF16)

    w_copies[0].wait()
    x_copies[1].start()
    for i, (first, height) in enumerate(X_BLOCKS):
        x_copies[i].wait()
        if i == 0:
            x_copies[2].start()
            x_copies[3].start()
            w_copies[1].start()
        if i == 1:
            w_copies[2].start()
            w_copies[3].start()
        rows = slice(first, first + height)
        block = jnp.dot(xv[rows], wr[...], preferred_element_type=F32)
        red[rows] = jnp.maximum(block, 0.0).astype(BF16)

    w_copies[1].wait()

    def forward(i, carry):
        cols = pl.ds(pl.multiple_of(i * CHUNK, CHUNK), CHUNK)
        pre = jnp.dot(red[:ROWS], we[:, cols], preferred_element_type=F32)
        pre = xv[:ROWS, cols].astype(F32) + pre
        mask[:ROWS, cols] = jnp.where(pre > 0, 1.0, 0.0).astype(BF16)
        feat[:, cols] = jnp.sum(jnp.maximum(pre, 0.0).reshape(POS, TILES, CHUNK), axis=0)
        return carry

    lax.fori_loop(0, D // CHUNK, forward, 0)

    features = (feat[...] / POS).astype(BF16)
    w_copies[2].wait()
    value = jnp.tanh(jnp.dot(features, av[...], preferred_element_type=F32))
    w_copies[3].wait()
    gate = jax.nn.sigmoid(jnp.dot(features, ag[...], preferred_element_type=F32))
    vector, classes = vec_ref[...], cls_ref[...]
    scores = jnp.sum(value * gate * vector, axis=1, keepdims=True)
    weight = jnp.exp(scores)
    along = jnp.sum(features.astype(F32) * classes, axis=1, keepdims=True)

    lane = lax.broadcasted_iota(jnp.int32, (TILES, 128), 1)
    square = (TILES, TILES)
    diagonal = lax.broadcasted_iota(jnp.int32, square, 0) == lax.broadcasted_iota(jnp.int32, square, 1)
    named = jnp.where(diagonal, jnp.broadcast_to(slide_ref[...].astype(F32), square), 0.0)
    named = jnp.sum(named, axis=1, keepdims=True)
    member = jnp.where(named == lane.astype(F32), 1.0, 0.0)
    lane_row = lax.broadcasted_iota(jnp.int32, (1, 128), 1)
    label_row = jnp.where(lane_row == place.slide, label_ref[0].astype(F32), 0.0)
    weight_row = jnp.sum(member * weight, axis=0, keepdims=True)
    along_row = jnp.sum(member * (weight * (along * 2.0**-8)), axis=0, keepdims=True)

    slots = (stat0, stat1, stat2)
    spots = (place.slide,) + place.at[1:]

    def stat_send(step):
        slot = slots[step].at[spots[step]]
        devices = [place.partner(step, ahead) for ahead in (1, 2, 3)]
        if step == 0:
            devices += [place.twin] + [place.across(ahead) for ahead in (1, 2, 3)]
        for device in devices:
            start_copy(slot, slot, stat_send_sem.at[step], stat_recv.at[step], device)

    def stat_sum(step):
        others = slots[step].at[pl.ds(0, slots[step].shape[0] - 1)]
        wait_bytes(others, stat_recv.at[step])
        wait_bytes(others, stat_send_sem.at[step])
        total = slots[step][0]
        for i in range(1, slots[step].shape[0]):
            total = total + slots[step][i]
        return total

    def transpose_x(first, last):
        def turn(i, carry):
            cols = pl.ds(pl.multiple_of(i * 256, 256), 256)
            xt[cols, :] = xv[:, cols].T
            return carry

        lax.fori_loop(first, last, turn, 0)

    def put(step, rows):
        slots[step][spots[step]] = rows

    stat_rows = jnp.concatenate([weight_row, along_row, label_row, jnp.zeros((5, 128), F32)], axis=0)
    put(0, stat_rows)
    pl.semaphore_wait(barrier, len(partners))
    stat_send(0)

    def split(cot):
        high = cot.astype(BF16)
        return jnp.concatenate([high, (cot - high.astype(F32)).astype(BF16)], axis=0)

    value_cot = split(vector * (1.0 - value * value) * gate)
    gate_cot = split(vector * value * gate * (1.0 - gate))

    def score_cols(i, carry):
        cols = pl.ds(pl.multiple_of(i * 512, 512), 512)
        both = lax.dot_general(value_cot, av[cols, :], NT, preferred_element_type=F32)
        both = both + lax.dot_general(gate_cot, ag[cols, :], NT, preferred_element_type=F32)
        score_part[:, cols] = both[:TILES] + both[TILES:]
        return carry

    lax.fori_loop(0, D // 512, score_cols, 0)
    put(1, stat_sum(0))
    stat_send(1)
    transpose_x(0, 8)
    put(2, stat_sum(1))
    stat_send(2)
    redt[...] = red[...].T
    totals = stat_sum(2)

    live = lane_row < 8
    weight_total = jnp.where(live, totals[0:1], 1.0)
    logits = jnp.where(live, totals[1:2], 0.0) / weight_total * 2.0**8
    labels = totals[2:3] / 16.0
    losses = jnp.maximum(logits, 0.0) + jnp.log1p(jnp.exp(-jnp.abs(logits))) - labels * logits
    loss = LOSS_SCALE * jnp.sum(jnp.where(live, losses, 0.0))
    own_logit = jnp.sum(jnp.where(lane_row == place.slide, logits, 0.0))
    stat_ref[0:1] = jnp.full((1, 128), own_logit, F32)
    stat_ref[1:2] = jnp.full((1, 128), loss, F32)
    stat_ref[2:8] = jnp.zeros((6, 128), F32)
    slope = LOSS_SCALE * (jax.nn.sigmoid(logits) - labels)

    def of_tile(row):
        return jnp.sum(member * row, axis=1, keepdims=True)

    share = weight / of_tile(weight_total)
    pull = share * of_tile(slope)
    score_grad = pull * (along - of_tile(logits))
    grad = (pull * classes + score_grad * score_part[...]).astype(BF16)
    scaled = (grad.astype(F32) / POS).astype(BF16)

    def mask_rows(i, carry):
        rows = pl.ds(pl.multiple_of(i * BLOCK, BLOCK), BLOCK)
        spread = jnp.broadcast_to(scaled[None], (BLOCK // TILES, TILES, D)).reshape(BLOCK, D)
        mask[rows] = mask[rows] * spread
        return carry

    lax.fori_loop(0, BLOCKS, mask_rows, 0)

    def e_out(p, k, rows):
        at = pl.ds(pl.multiple_of(k * rows, rows), rows)
        return ge_ref.at[at, pl.ds(pl.multiple_of(core * HALF + p * E_WIDTH, E_WIDTH), E_WIDTH)]

    def r_out(p, k, rows):
        at = pl.ds(pl.multiple_of(p * 4 * R_SHARD + k * rows, rows), rows)
        return gr_ref.at[at, pl.ds(pl.multiple_of(core * CHUNK, CHUNK), CHUNK)]

    e_sum = Sum(place, E_SHIFT, E_SHARD, e_out, (send_e, acc_e, got_e), part_bufs[:4], recv_e, done_e)
    r_sum = Sum(place, R_SHIFT, R_SHARD, r_out, (send_r, acc_r, got_r), part_bufs[4:], recv_r, done_r)

    def expand(turn, i, halves=1):
        store = send_e if turn else acc_e
        half = lax.rem(core + turn, 2)
        cols = pl.ds(pl.multiple_of(half * HALF + i * CHUNK, CHUNK), CHUNK)
        rows = MID // halves
        for j in range(halves):
            out = jnp.dot(redt[j * rows : (j + 1) * rows], mask[:, cols], preferred_element_type=F32).astype(BF16)
            store[pl.ds(2 * i * MID + j * rows, rows)] = out[:, :E_WIDTH]
            store[pl.ds((2 * i + 1) * MID + j * rows, rows)] = out[:, E_WIDTH:]

    def back():
        for half in (0, 1):
            cols = slice(half * CHUNK, (half + 1) * CHUNK)
            proj = lax.dot_general(mask[:ROWS], we[cols], NT, preferred_element_type=F32)
            rg[half, :ROWS] = jnp.where(red[:ROWS, cols] > 0, proj, 0.0).astype(BF16)

    def reduce(turn, i, halves=1):
        store = send_r if turn else acc_r
        half = lax.rem(core + turn, 2)
        height = 512 // halves
        for j in range(halves):
            rows = slice(i * 512 + j * height, i * 512 + (j + 1) * height)
            store[rows] = jnp.dot(xt[rows], rg[half], preferred_element_type=F32).astype(BF16)

    expand(1, 0, 2)
    e_sum.send_twin(0)
    for i in range(3):
        expand(0, i)
        expand(1, i + 1)
        e_sum.send_twin(i + 1)
        e_sum.send_a(i)
    expand(0, 3, 2)
    e_sum.send_a(3)
    back()
    e_sum.send_b(0)
    reduce(1, 0, 2)
    r_sum.send_twin(0)
    for i in range(3):
        e_sum.send_b(i + 1)
        reduce(0, i)
        reduce(1, i + 1)
        r_sum.send_twin(i + 1)
        r_sum.send_a(i)
        if i > 0:
            e_sum.send_c(i - 1)
    reduce(0, 3, 2)
    r_sum.send_a(3)

    starts = (
        (0.4, r_sum.send_b),
        (4.0, r_sum.send_c),
        (7.6, r_sum.gather_b),
        (11.2, r_sum.gather_a),
        (16.0, r_sum.hand_on),
        (-2.5, e_sum.send_c),
        (1.0, e_sum.gather_b),
        (4.6, e_sum.gather_a),
        (11.4, e_sum.hand_on),
    )
    events = [(at + 1.4 * k, n, k) for n, (at, _) in enumerate(starts) for k in range(4)]
    events.append((EXPAND_DONE, len(starts), 0))
    for at, n, k in sorted(events):
        if n == len(starts):
            for i in range(4):
                e_sum.finish(i)
            scale = inverse_rms(ge_ref)
            for i in range(0, MID, 64):
                ge_ref[i : i + 64] = (ge_ref[i : i + 64].astype(F32) * scale).astype(BF16)
        elif starts[n][1] != e_sum.send_c or k > 1:
            starts[n][1](k)
    for k in range(4):
        r_sum.finish(k)


def pooled_gradients(x, wr, we, av, ag, vector, classes, slides, labels):
    any_space = pl.BlockSpec(memory_space=pl.ANY)
    vmem = pl.BlockSpec(memory_space=pltpu.VMEM)
    smem = pl.BlockSpec(memory_space=pltpu.SMEM)
    scratch = [
        pltpu.VMEM((PADDED, D), BF16),
        pltpu.VMEM((D, MID), BF16),
        pltpu.VMEM((MID, D), BF16),
        pltpu.VMEM((D, ATT), BF16),
        pltpu.VMEM((D, ATT), BF16),
        pltpu.VMEM((PADDED, MID), BF16),
        pltpu.VMEM((PADDED, D), BF16),
        pltpu.VMEM((D, PADDED), BF16),
        pltpu.VMEM((MID, PADDED), BF16),
        pltpu.VMEM((2, PADDED, MID // 2), BF16),
        pltpu.VMEM((TILES, D), F32),
        pltpu.VMEM((TILES, D), F32),
    ]
    scratch += [pltpu.VMEM((E_COUNT * MID, E_WIDTH), BF16)] * 3
    scratch += [pltpu.VMEM((D, MID // 2), BF16)] * 3
    scratch += [pltpu.VMEM((n, 8, 128), F32) for n in (8, 4, 4)]
    scratch += [
        pltpu.SemaphoreType.DMA((len(X_BLOCKS),)),
        pltpu.SemaphoreType.DMA((4,)),
        pltpu.SemaphoreType.DMA((4,)),
        pltpu.SemaphoreType.DMA((4,)),
        pltpu.SemaphoreType.DMA((4, 7)),
        pltpu.SemaphoreType.DMA((4, 7)),
        pltpu.SemaphoreType.DMA((4,)),
        pltpu.SemaphoreType.DMA((4,)),
    ]
    scratch += part_scratch(E_COUNT, E_SHARD, E_WIDTH)
    scratch += part_scratch(R_COUNT, R_SHARD, CHUNK)
    return pl.pallas_call(
        body,
        name="pooled_gradients",
        out_shape=(
            pltpu.VMEM((MID, D), BF16),
            pltpu.VMEM((D, MID), BF16),
            pltpu.VMEM((8, 128), F32),
        ),
        in_specs=[any_space] * 5 + [vmem] * 3 + [smem],
        out_specs=(vmem, vmem, vmem),
        scratch_shapes=scratch,
        cost_estimate=pl.CostEstimate(flops=17_000_000_000, bytes_accessed=24_000_000, transcendentals=70_000),
        compiler_params=pltpu.CompilerParams(
            collective_id=0, has_side_effects=True, vmem_limit_bytes=54 * 2**20
        ),
    )(x, wr, we, av, ag, vector, classes, slides, labels)


def normalize_body(ue_ref, gr_ref, stat_ref, ue_hbm, ur_hbm, logit_ref, loss_ref, ur, sems):
    whole = pltpu.make_async_copy(ue_ref, ue_hbm, sems.at[0])
    whole.start()
    scale = inverse_rms(gr_ref)
    rows = D // 4
    copies = [whole]
    for i in range(4):
        at = pl.ds(i * rows, rows)
        ur[at] = (gr_ref[at].astype(F32) * scale).astype(BF16)
        copies.append(pltpu.make_async_copy(ur.at[at], ur_hbm.at[at], sems.at[1 + i]))
        copies[-1].start()
    logit_ref[0] = stat_ref[0, 0]
    loss_ref[0] = stat_ref[1, 0]
    for copy in copies:
        copy.wait()


def normalize(ue, gr, stat):
    any_space = pl.BlockSpec(memory_space=pl.ANY)
    vmem = pl.BlockSpec(memory_space=pltpu.VMEM)
    smem = pl.BlockSpec(memory_space=pltpu.SMEM)
    return pl.pallas_call(
        normalize_body,
        name="normalize",
        out_shape=(
            jax.ShapeDtypeStruct((MID, D), BF16),
            jax.ShapeDtypeStruct((D, MID), BF16),
            jax.ShapeDtypeStruct((1,), F32),
            jax.ShapeDtypeStruct((1,), F32),
        ),
        in_specs=[vmem, vmem, vmem],
        out_specs=(any_space, any_space, smem, smem),
        scratch_shapes=[pltpu.VMEM((D, MID), BF16), pltpu.SemaphoreType.DMA((5,))],
        compiler_params=pltpu.CompilerParams(vmem_limit_bytes=16 * 2**20),
    )(ue, gr, stat)


def shards(
    features_in, w_reduce, w_expand, att_value, att_gate, att_vector, classifier, tile_slide, labels
):
    rows = features_in.transpose(1, 0, 2).reshape(ROWS, D)
    ge, gr, stat = pooled_gradients(
        rows, w_reduce, w_expand, att_value, att_gate,
        att_vector.reshape(1, ATT), classifier.reshape(1, D), tile_slide.reshape(1, TILES), labels,
    )
    update_expand, update_reduce, logit, loss = normalize(ge, gr, stat)
    return (update_reduce, update_expand, logit, loss.reshape(()))


def solution(mesh):
    placed = (
        P(("tile", "slide"), None, None),
        P(),
        P(),
        P(),
        P(),
        P(),
        P(),
        P(("tile", "slide"), None),
        P("slide"),
    )
    return jax.shard_map(
        shards, mesh=mesh, in_specs=placed, out_specs=(P(), P(), P("slide"), P()), check_vma=False
    )
```

```python
import functools

import jax
import jax.numpy as jnp
from jax import lax
from jax.experimental import pallas as pl
from jax.experimental.pallas import tpu as pltpu
from jax.sharding import PartitionSpec as P

LOSS_SCALE = 1024.0
MESH = pl.DeviceIdType.MESH
F32, BF16 = jnp.float32, jnp.bfloat16
TILES, POS, D, MID, ATT = 32, 49, 2048, 512, 1024
ROWS = TILES * POS
PADDED = 1664
BLOCK = 224
BLOCKS = ROWS // BLOCK
X_BLOCKS = ((0, 416), (416, 384), (800, 384), (1184, 384))
CHUNK = 256
HALF = D // 2
E_COUNT, E_SHARD, E_SHIFT, E_WIDTH = 8, 128, 0, 128
R_COUNT, R_SHARD, R_SHIFT = 8, 64, 1
TWIN, LINE_A, LINE_B, LINE_C, BACK_B, BACK_A, HAND = range(7)
NT = (((1,), (1,)), ((), ()))
EXPAND_DONE = 16.1


class Place:
    def __init__(self):
        self.tile, self.slide = lax.axis_index("tile"), lax.axis_index("slide")
        self.core = lax.rem(self.slide, 2)
        self.at = (lax.div(self.slide, 2), lax.rem(self.tile, 4), lax.div(self.tile, 4))
        self.twin = (self.tile, self.slide + 1 - 2 * self.core)
        self.ahead = [[lax.rem(c + step, 4) for step in range(4)] for c in self.at]

    def across(self, step):
        tile, slide = self.partner(0, step)
        return (tile, slide + 1 - 2 * self.core)

    def partner(self, axis, step):
        x, y, z = (self.ahead[a][step] if a == axis else c for a, c in enumerate(self.at))
        return (z * 4 + y, x * 2 + self.core)


def start_copy(src, dst, send_sem, recv_sem, device):
    pltpu.make_async_remote_copy(
        src_ref=src, dst_ref=dst, send_sem=send_sem, recv_sem=recv_sem, device_id=device, device_id_type=MESH
    ).start()


def wait_bytes(like, sem):
    pltpu.make_async_copy(like, like, sem).wait()


class Sum:
    def __init__(self, place, shift, shard, out_part, near, bufs, recv, send):
        self.place, self.shift, self.shard_rows, self.out_part = place, shift, shard, out_part
        self.theirs, self.mine, self.got = near
        self.recv_a, self.sum_a, self.recv_b, self.all_c = bufs
        self.recv, self.send = recv, send

    def axis(self, p, turn):
        return (p + self.shift + turn) % 3

    def shard(self, p, k):
        rows = self.shard_rows
        return pl.ds(pl.multiple_of((p * 4 + k) * rows, rows), rows)

    def quarter(self, k):
        rows = self.shard_rows // 4
        return pl.ds(pl.multiple_of(k * rows, rows), rows)

    def part(self, p):
        rows = 4 * self.shard_rows
        return pl.ds(p * rows, rows)

    def whole(self, k):
        rows = 8 * self.shard_rows
        return pl.ds(k * rows, rows)

    def shards(self, k):
        return self.recv_a.at[pl.ds(2 * k, 2)]

    def quarters(self, k):
        return self.recv_b.at[pl.ds(2 * k, 2)]

    def to_line(self, p, stage, axis, src, dst):
        k = p // 2
        for step in (1, 2, 3):
            start_copy(src(step), dst(step), self.send.at[k], self.recv.at[k, stage], self.place.partner(axis, step))

    def to_twin(self, k, stage, src, dst):
        start_copy(src, dst, self.send.at[k], self.recv.at[k, stage], self.place.twin)

    def send_twin(self, k):
        rows = self.whole(k)
        self.to_twin(k, TWIN, self.theirs.at[rows], self.got.at[rows])

    def send_a(self, k):
        rows = self.whole(k)
        wait_bytes(self.got.at[rows], self.recv.at[k, TWIN])
        self.mine[rows] = (self.mine[rows].astype(F32) + self.got[rows].astype(F32)).astype(BF16)
        wait_bytes(self.theirs.at[rows], self.send.at[k])
        for p in (2 * k, 2 * k + 1):
            axis = self.axis(p, 0)
            self.to_line(
                p, LINE_A, axis,
                lambda step: self.mine.at[self.shard(p, self.place.ahead[axis][step])],
                lambda step: self.recv_a.at[p, step - 1],
            )

    def send_b(self, k):
        wait_bytes(self.shards(k), self.recv.at[k, LINE_A])
        wait_bytes(self.shards(k), self.send.at[k])
        for p in (2 * k, 2 * k + 1):
            total = self.mine[self.shard(p, self.place.at[self.axis(p, 0)])].astype(F32)
            for i in range(3):
                total = total + self.recv_a[p, i].astype(F32)
            self.sum_a[p] = total.astype(BF16)
            axis = self.axis(p, 1)
            self.to_line(
                p, LINE_B, axis,
                lambda step: self.sum_a.at[p, self.quarter(self.place.ahead[axis][step])],
                lambda step: self.recv_b.at[p, step - 1],
            )

    def send_c(self, k):
        wait_bytes(self.quarters(k), self.recv.at[k, LINE_B])
        wait_bytes(self.quarters(k), self.send.at[k])
        for p in (2 * k, 2 * k + 1):
            total = self.sum_a[p, self.quarter(self.place.at[self.axis(p, 1)])].astype(F32)
            for i in range(3):
                total = total + self.recv_b[p, i].astype(F32)
            axis = self.axis(p, 2)
            slot = self.all_c.at[p, self.place.at[axis]]
            slot[...] = total.astype(BF16)
            self.to_line(p, LINE_C, axis, lambda step: slot, lambda step: slot)

    def gather_b(self, k):
        wait_bytes(self.quarters(k), self.recv.at[k, LINE_C])
        wait_bytes(self.quarters(k), self.send.at[k])
        for p in (2 * k, 2 * k + 1):
            total = self.all_c[p, 0].astype(F32)
            for i in (1, 2, 3):
                total = total + self.all_c[p, i].astype(F32)
            axis = self.axis(p, 1)
            rows = self.shard_rows // 4
            own = self.out_part(p, self.place.at[self.axis(p, 0)] * 4 + self.place.at[axis], rows)
            own[...] = total.astype(BF16)
            self.to_line(p, BACK_B, axis, lambda step: own, lambda step: own)

    def gather_a(self, k):
        wait_bytes(self.quarters(k), self.recv.at[k, BACK_B])
        wait_bytes(self.quarters(k), self.send.at[k])
        for p in (2 * k, 2 * k + 1):
            axis = self.axis(p, 0)
            own = self.out_part(p, self.place.at[axis], self.shard_rows)
            self.to_line(p, BACK_A, axis, lambda step: own, lambda step: own)
        for p in (2 * k, 2 * k + 1):
            own = self.out_part(p, self.place.at[self.axis(p, 0)], self.shard_rows)
            self.to_twin(k, HAND, own, own)

    def hand_on(self, k):
        wait_bytes(self.shards(k), self.recv.at[k, BACK_A])
        wait_bytes(self.mine.at[self.whole(k)], self.send.at[k])
        for p in (2 * k, 2 * k + 1):
            for step in (1, 2, 3):
                block = self.out_part(p, self.place.ahead[self.axis(p, 0)][step], self.shard_rows)
                self.to_twin(k, HAND, block, block)

    def finish(self, k):
        wait_bytes(self.mine.at[self.whole(k)], self.recv.at[k, HAND])
        wait_bytes(self.shards(k), self.send.at[k])


def inverse_rms(ref):
    height, width = ref.shape
    total = jnp.zeros((8, width), F32)
    for i in range(0, height, 64):
        values = ref[i : i + 64].astype(F32)
        total = total + jnp.sum((values * values).reshape(8, 8, width), axis=0)
    mean = jnp.sum(total) / (D * MID)
    return 1.0 / jnp.sqrt(jnp.full((1, width), mean + 1e-06, F32))


def part_scratch(count, rows, width):
    quarter = rows // 4
    shapes = [(3, rows), (rows,), (3, quarter), (4, quarter)]
    return [pltpu.VMEM((count,) + shape + (width,), BF16) for shape in shapes]


def body(
    x_hbm, wr_hbm, we_hbm, av_hbm, ag_hbm, vec_ref, cls_ref, slide_ref, label_ref,
    ge_ref, gr_ref, stat_ref,
    xv, wr, we, av, ag, red, mask, xt, redt, rg, feat, score_part, scaled_ref,
    send_e, acc_e, got_e, send_r, acc_r, got_r, stat0, stat1, stat2,
    x_sem, w_sem, stat_recv, stat_send_sem, recv_e, recv_r, done_e, done_r, *part_bufs,
):
    place = Place()
    core = place.core

    x_copies = [
        pltpu.make_async_copy(x_hbm.at[pl.ds(first, rows)], xv.at[pl.ds(first, rows)], x_sem.at[i])
        for i, (first, rows) in enumerate(X_BLOCKS)
    ]
    weights = ((wr_hbm, wr), (we_hbm, we), (av_hbm, av), (ag_hbm, ag))
    w_copies = [pltpu.make_async_copy(a, b, w_sem.at[i]) for i, (a, b) in enumerate(weights)]
    w_copies[0].start()
    x_copies[0].start()

    barrier = pltpu.get_barrier_semaphore()
    partners = [place.twin] + [place.partner(axis, step) for axis in range(3) for step in (1, 2, 3)]
    partners += [place.across(step) for step in (1, 2, 3)]
    for device in partners:
        pl.semaphore_signal(barrier, inc=1, device_id=device, device_id_type=MESH)

    tail = PADDED - ROWS
    xv[ROWS:] = jnp.zeros((tail, D), BF16)
    red[ROWS:] = jnp.zeros((tail, MID), BF16)
    mask[ROWS:] = jnp.zeros((tail, D), BF16)
    rg[:, ROWS:] = jnp.zeros((2, tail, MID // 2), BF16)

    w_copies[0].wait()
    x_copies[1].start()
    for i, (first, height) in enumerate(X_BLOCKS):
        x_copies[i].wait()
        if i == 0:
            x_copies[2].start()
            x_copies[3].start()
            w_copies[1].start()
        if i == 1:
            w_copies[2].start()
            w_copies[3].start()
        rows = slice(first, first + height)
        block = jnp.dot(xv[rows], wr[...], preferred_element_type=F32)
        red[rows] = jnp.maximum(block, 0.0).astype(BF16)

    w_copies[1].wait()

    def forward(i, carry):
        cols = pl.ds(pl.multiple_of(i * CHUNK, CHUNK), CHUNK)
        pre = jnp.dot(red[:ROWS], we[:, cols], preferred_element_type=F32)
        pre = xv[:ROWS, cols].astype(F32) + pre
        mask[:ROWS, cols] = jnp.where(pre > 0, 1.0, 0.0).astype(BF16)
        feat[:, cols] = jnp.sum(jnp.maximum(pre, 0.0).reshape(POS, TILES, CHUNK), axis=0)
        return carry

    lax.fori_loop(0, D // CHUNK, forward, 0)

    features = (feat[...] / POS).astype(BF16)
    w_copies[2].wait()
    value = jnp.tanh(jnp.dot(features, av[...], preferred_element_type=F32))
    w_copies[3].wait()
    gate = jax.nn.sigmoid(jnp.dot(features, ag[...], preferred_element_type=F32))
    vector, classes = vec_ref[...], cls_ref[...]
    scores = jnp.sum(value * gate * vector, axis=1, keepdims=True)
    weight = jnp.exp(scores)
    along = jnp.sum(features.astype(F32) * classes, axis=1, keepdims=True)

    lane = lax.broadcasted_iota(jnp.int32, (TILES, 128), 1)
    square = (TILES, TILES)
    diagonal = lax.broadcasted_iota(jnp.int32, square, 0) == lax.broadcasted_iota(jnp.int32, square, 1)
    named = jnp.where(diagonal, jnp.broadcast_to(slide_ref[...].astype(F32), square), 0.0)
    named = jnp.sum(named, axis=1, keepdims=True)
    member = jnp.where(named == lane.astype(F32), 1.0, 0.0)
    lane_row = lax.broadcasted_iota(jnp.int32, (1, 128), 1)
    label_row = jnp.where(lane_row == place.slide, label_ref[0].astype(F32), 0.0)
    weight_row = jnp.sum(member * weight, axis=0, keepdims=True)
    along_row = jnp.sum(member * (weight * (along * 2.0**-8)), axis=0, keepdims=True)

    slots = (stat0, stat1, stat2)
    spots = (place.slide,) + place.at[1:]

    def stat_send(step):
        slot = slots[step].at[spots[step]]
        devices = [place.partner(step, ahead) for ahead in (1, 2, 3)]
        if step == 0:
            devices += [place.twin] + [place.across(ahead) for ahead in (1, 2, 3)]
        for device in devices:
            start_copy(slot, slot, stat_send_sem.at[step], stat_recv.at[step], device)

    def stat_sum(step):
        others = slots[step].at[pl.ds(0, slots[step].shape[0] - 1)]
        wait_bytes(others, stat_recv.at[step])
        wait_bytes(others, stat_send_sem.at[step])
        total = slots[step][0]
        for i in range(1, slots[step].shape[0]):
            total = total + slots[step][i]
        return total

    def transpose_x(first, last):
        def turn(i, carry):
            cols = pl.ds(pl.multiple_of(i * 256, 256), 256)
            xt[cols, :] = xv[:, cols].T
            return carry

        lax.fori_loop(first, last, turn, 0)

    def put(step, rows):
        slots[step][spots[step]] = rows

    stat_rows = jnp.concatenate([weight_row, along_row, label_row, jnp.zeros((5, 128), F32)], axis=0)
    put(0, stat_rows)
    pl.semaphore_wait(barrier, len(partners))
    stat_send(0)

    def split(cot):
        high = cot.astype(BF16)
        return jnp.concatenate([high, (cot - high.astype(F32)).astype(BF16)], axis=0)

    value_cot = split(vector * (1.0 - value * value) * gate)
    gate_cot = split(vector * value * gate * (1.0 - gate))

    def score_cols(i, carry):
        cols = pl.ds(pl.multiple_of(i * 512, 512), 512)
        both = lax.dot_general(value_cot, av[cols, :], NT, preferred_element_type=F32)
        both = both + lax.dot_general(gate_cot, ag[cols, :], NT, preferred_element_type=F32)
        score_part[:, cols] = both[:TILES] + both[TILES:]
        return carry

    lax.fori_loop(0, D // 512, score_cols, 0)
    put(1, stat_sum(0))
    stat_send(1)
    transpose_x(0, 8)
    put(2, stat_sum(1))
    stat_send(2)
    redt[...] = red[...].T
    totals = stat_sum(2)

    live = lane_row < 8
    weight_total = jnp.where(live, totals[0:1], 1.0)
    logits = jnp.where(live, totals[1:2], 0.0) / weight_total * 2.0**8
    labels = totals[2:3] / 16.0
    losses = jnp.maximum(logits, 0.0) + jnp.log1p(jnp.exp(-jnp.abs(logits))) - labels * logits
    loss = LOSS_SCALE * jnp.sum(jnp.where(live, losses, 0.0))
    own_logit = jnp.sum(jnp.where(lane_row == place.slide, logits, 0.0))
    stat_ref[0:1] = jnp.full((1, 128), own_logit, F32)
    stat_ref[1:2] = jnp.full((1, 128), loss, F32)
    stat_ref[2:8] = jnp.zeros((6, 128), F32)
    slope = LOSS_SCALE * (jax.nn.sigmoid(logits) - labels)

    def of_tile(row):
        return jnp.sum(member * row, axis=1, keepdims=True)

    share = weight / of_tile(weight_total)
    pull = share * of_tile(slope)
    score_grad = pull * (along - of_tile(logits))
    grad = (pull * classes + score_grad * score_part[...]).astype(BF16)
    scaled = (grad.astype(F32) / POS).astype(BF16)

    scaled_ref[...] = scaled

    def mask_cols(turn, i):
        half = lax.rem(core + turn, 2)
        cols = pl.ds(pl.multiple_of(half * HALF + i * CHUNK, CHUNK), CHUNK)
        spread = jnp.broadcast_to(scaled_ref[:, cols][None], (POS, TILES, CHUNK)).reshape(ROWS, CHUNK)
        mask[:ROWS, cols] = mask[:ROWS, cols] * spread

    def e_out(p, k, rows):
        at = pl.ds(pl.multiple_of(k * rows, rows), rows)
        return ge_ref.at[at, pl.ds(pl.multiple_of(core * HALF + p * E_WIDTH, E_WIDTH), E_WIDTH)]

    def r_out(p, k, rows):
        at = pl.ds(pl.multiple_of(p * 4 * R_SHARD + k * rows, rows), rows)
        return gr_ref.at[at, pl.ds(pl.multiple_of(core * CHUNK, CHUNK), CHUNK)]

    e_sum = Sum(place, E_SHIFT, E_SHARD, e_out, (send_e, acc_e, got_e), part_bufs[:4], recv_e, done_e)
    r_sum = Sum(place, R_SHIFT, R_SHARD, r_out, (send_r, acc_r, got_r), part_bufs[4:], recv_r, done_r)

    def expand(turn, i, halves=1):
        store = send_e if turn else acc_e
        half = lax.rem(core + turn, 2)
        cols = pl.ds(pl.multiple_of(half * HALF + i * CHUNK, CHUNK), CHUNK)
        rows = MID // halves
        for j in range(halves):
            out = jnp.dot(redt[j * rows : (j + 1) * rows], mask[:, cols], preferred_element_type=F32).astype(BF16)
            store[pl.ds(2 * i * MID + j * rows, rows)] = out[:, :E_WIDTH]
            store[pl.ds((2 * i + 1) * MID + j * rows, rows)] = out[:, E_WIDTH:]

    def back():
        for half in (0, 1):
            cols = slice(half * CHUNK, (half + 1) * CHUNK)
            proj = lax.dot_general(mask[:ROWS], we[cols], NT, preferred_element_type=F32)
            rg[half, :ROWS] = jnp.where(red[:ROWS, cols] > 0, proj, 0.0).astype(BF16)

    def reduce(turn, i, halves=1):
        store = send_r if turn else acc_r
        half = lax.rem(core + turn, 2)
        height = 512 // halves
        for j in range(halves):
            rows = slice(i * 512 + j * height, i * 512 + (j + 1) * height)
            store[rows] = jnp.dot(xt[rows], rg[half], preferred_element_type=F32).astype(BF16)

    mask_cols(1, 0)
    expand(1, 0, 2)
    mask_cols(0, 0)
    mask_cols(1, 1)
    e_sum.send_twin(0)
    for i in range(3):
        expand(0, i)
        expand(1, i + 1)
        mask_cols(0, i + 1)
        if i < 2:
            mask_cols(1, i + 2)
        e_sum.send_twin(i + 1)
        e_sum.send_a(i)
    expand(0, 3, 2)
    e_sum.send_a(3)
    back()
    e_sum.send_b(0)
    reduce(1, 0, 2)
    r_sum.send_twin(0)
    for i in range(3):
        e_sum.send_b(i + 1)
        reduce(0, i)
        reduce(1, i + 1)
        r_sum.send_twin(i + 1)
        r_sum.send_a(i)
        if i > 0:
            e_sum.send_c(i - 1)
    reduce(0, 3, 2)
    r_sum.send_a(3)

    starts = (
        (0.4, r_sum.send_b),
        (4.0, r_sum.send_c),
        (7.6, r_sum.gather_b),
        (11.2, r_sum.gather_a),
        (16.0, r_sum.hand_on),
        (-2.5, e_sum.send_c),
        (1.0, e_sum.gather_b),
        (4.6, e_sum.gather_a),
        (11.4, e_sum.hand_on),
    )
    events = [(at + 1.4 * k, n, k) for n, (at, _) in enumerate(starts) for k in range(4)]
    events.append((EXPAND_DONE, len(starts), 0))
    for at, n, k in sorted(events):
        if n == len(starts):
            for i in range(4):
                e_sum.finish(i)
            scale = inverse_rms(ge_ref)
            for i in range(0, MID, 64):
                ge_ref[i : i + 64] = (ge_ref[i : i + 64].astype(F32) * scale).astype(BF16)
        elif starts[n][1] != e_sum.send_c or k > 1:
            starts[n][1](k)
    for k in range(4):
        r_sum.finish(k)


def pooled_gradients(x, wr, we, av, ag, vector, classes, slides, labels):
    any_space = pl.BlockSpec(memory_space=pl.ANY)
    vmem = pl.BlockSpec(memory_space=pltpu.VMEM)
    smem = pl.BlockSpec(memory_space=pltpu.SMEM)
    scratch = [
        pltpu.VMEM((PADDED, D), BF16),
        pltpu.VMEM((D, MID), BF16),
        pltpu.VMEM((MID, D), BF16),
        pltpu.VMEM((D, ATT), BF16),
        pltpu.VMEM((D, ATT), BF16),
        pltpu.VMEM((PADDED, MID), BF16),
        pltpu.VMEM((PADDED, D), BF16),
        pltpu.VMEM((D, PADDED), BF16),
        pltpu.VMEM((MID, PADDED), BF16),
        pltpu.VMEM((2, PADDED, MID // 2), BF16),
        pltpu.VMEM((TILES, D), F32),
        pltpu.VMEM((TILES, D), F32),
        pltpu.VMEM((TILES, D), BF16),
    ]
    scratch += [pltpu.VMEM((E_COUNT * MID, E_WIDTH), BF16)] * 3
    scratch += [pltpu.VMEM((D, MID // 2), BF16)] * 3
    scratch += [pltpu.VMEM((n, 8, 128), F32) for n in (8, 4, 4)]
    scratch += [
        pltpu.SemaphoreType.DMA((len(X_BLOCKS),)),
        pltpu.SemaphoreType.DMA((4,)),
        pltpu.SemaphoreType.DMA((4,)),
        pltpu.SemaphoreType.DMA((4,)),
        pltpu.SemaphoreType.DMA((4, 7)),
        pltpu.SemaphoreType.DMA((4, 7)),
        pltpu.SemaphoreType.DMA((4,)),
        pltpu.SemaphoreType.DMA((4,)),
    ]
    scratch += part_scratch(E_COUNT, E_SHARD, E_WIDTH)
    scratch += part_scratch(R_COUNT, R_SHARD, CHUNK)
    return pl.pallas_call(
        body,
        name="pooled_gradients",
        out_shape=(
            pltpu.VMEM((MID, D), BF16),
            pltpu.VMEM((D, MID), BF16),
            pltpu.VMEM((8, 128), F32),
        ),
        in_specs=[any_space] * 5 + [vmem] * 3 + [smem],
        out_specs=(vmem, vmem, vmem),
        scratch_shapes=scratch,
        cost_estimate=pl.CostEstimate(flops=17_000_000_000, bytes_accessed=24_000_000, transcendentals=70_000),
        compiler_params=pltpu.CompilerParams(
            collective_id=0, has_side_effects=True, vmem_limit_bytes=54 * 2**20
        ),
    )(x, wr, we, av, ag, vector, classes, slides, labels)


def normalize_body(ue_ref, gr_ref, stat_ref, ue_hbm, ur_hbm, logit_ref, loss_ref, ur, sems):
    whole = pltpu.make_async_copy(ue_ref, ue_hbm, sems.at[0])
    whole.start()
    scale = inverse_rms(gr_ref)
    rows = D // 4
    copies = [whole]
    for i in range(4):
        at = pl.ds(i * rows, rows)
        ur[at] = (gr_ref[at].astype(F32) * scale).astype(BF16)
        copies.append(pltpu.make_async_copy(ur.at[at], ur_hbm.at[at], sems.at[1 + i]))
        copies[-1].start()
    logit_ref[0] = stat_ref[0, 0]
    loss_ref[0] = stat_ref[1, 0]
    for copy in copies:
        copy.wait()


def normalize(ue, gr, stat):
    any_space = pl.BlockSpec(memory_space=pl.ANY)
    vmem = pl.BlockSpec(memory_space=pltpu.VMEM)
    smem = pl.BlockSpec(memory_space=pltpu.SMEM)
    return pl.pallas_call(
        normalize_body,
        name="normalize",
        out_shape=(
            jax.ShapeDtypeStruct((MID, D), BF16),
            jax.ShapeDtypeStruct((D, MID), BF16),
            jax.ShapeDtypeStruct((1,), F32),
            jax.ShapeDtypeStruct((1,), F32),
        ),
        in_specs=[vmem, vmem, vmem],
        out_specs=(any_space, any_space, smem, smem),
        scratch_shapes=[pltpu.VMEM((D, MID), BF16), pltpu.SemaphoreType.DMA((5,))],
        compiler_params=pltpu.CompilerParams(vmem_limit_bytes=16 * 2**20),
    )(ue, gr, stat)


def shards(
    features_in, w_reduce, w_expand, att_value, att_gate, att_vector, classifier, tile_slide, labels
):
    rows = features_in.transpose(1, 0, 2).reshape(ROWS, D)
    ge, gr, stat = pooled_gradients(
        rows, w_reduce, w_expand, att_value, att_gate,
        att_vector.reshape(1, ATT), classifier.reshape(1, D), tile_slide.reshape(1, TILES), labels,
    )
    update_expand, update_reduce, logit, loss = normalize(ge, gr, stat)
    return (update_reduce, update_expand, logit, loss.reshape(()))


def solution(mesh):
    placed = (
        P(("tile", "slide"), None, None),
        P(),
        P(),
        P(),
        P(),
        P(),
        P(),
        P(("tile", "slide"), None),
        P("slide"),
    )
    return jax.shard_map(
        shards, mesh=mesh, in_specs=placed, out_specs=(P(), P(), P("slide"), P()), check_vma=False
    )
```
